256 devices in a mesh: dp: 8 (over y, core), rows: 32 (over x, z).
Axes of the slice: x: 4, y: 4, z: 8, core: 2. Of those that a mesh axis runs over, the one named last changes fastest.
Arguments:
- image_tokens: bfloat16 [8, 256, 32, 512], P('dp', 'rows'), may hold values from -6 to 6
- top_cond: float32 [8, 512], P('dp'), may hold values from 0.5 to 2
- bottom_cond: float32 [8, 1024], P('dp'), may hold values from 0.5 to 2
- top_qkv: bfloat16 [512, 1536], P('rows'), may hold values from -0.25 to 0.25
- top_scale: float32 [8], replicated, may hold values from 4 to 16
- merge_weight: bfloat16 [2048, 1024], P('rows'), may hold values from -0.125 to 0.125
- bottom_qkv: bfloat16 [1024, 3072], P('rows'), may hold values from -0.1875 to 0.1875
- bottom_scale: float32 [16], replicated, may hold values from 4 to 16
- out_cotangent: bfloat16 [8, 128, 16, 1024], P('dp', 'rows'), may hold values from -6 to 6
Outputs:
- output: bfloat16 [8, 128, 16, 1024], P('dp', 'rows')
- grad_tokens: bfloat16 [8, 256, 32, 512], P('dp', 'rows')
- top_qkv_grad: float32 [512, 1536], P('rows', 'dp')
- merge_grad: float32 [2048, 1024], P('rows', 'dp')
- low_qkv_grad: float32 [1024, 3072], P('rows', 'dp')
The draws below stay inside these ranges and needn't reach their ends.
All inputs are finite; a program needn't handle non-finite values.
Results may differ from the reference program's by a relative error of at most 0.035.
Values may be sent and summed in bfloat16 or wider, within the bound.
No kernel may reach another device: no remote copies, remote signals or barrier semaphores. Data moves between devices by JAX's collectives and lax.ppermute only.
A program may use at most 192 MiB of HBM per device.

```python
import math
import jax
import jax.numpy as jnp
from jax import lax

C1 = 512
C2 = 1024
HEAD = 64
W1 = 32
IMAGES = 8
H1 = 256
H2 = 128
W2 = 16
N_ROWS = 32


def shard_levels(key, dims, shards, low, high):
    factor_of, own = 1.0, jax.random.fold_in(key, 6)
    for axis_at, shards_of in shards:
        steps = jnp.exp(jax.random.uniform(jax.random.fold_in(own, axis_at), (shards_of,), jnp.float32, low / len(shards), high / len(shards)))
        factor_of = factor_of * jnp.repeat(steps, dims[axis_at] // shards_of).reshape([-1 if axis == axis_at else 1 for axis in range(len(dims))])
    return factor_of


def bell_draw(stream_key, dims, width, most, pieces=(), kind=jnp.bfloat16):
    loudness = shard_levels(stream_key, dims, pieces, -0.22, 0.18) if pieces else 1.0
    drawn = jax.random.normal(stream_key, dims, jnp.float32) * width * loudness
    return jnp.minimum(jnp.maximum(drawn, -most), most).astype(kind)


def setup_inputs(seed: int = 0) -> dict:
    streams_of = jax.random.split(jax.random.key(seed), 10)
    image_tokens = bell_draw(streams_of[0], (IMAGES, H1, W1, C1), 1.0, 6.0, ((0, 8), (1, 32)))
    top_cond = jnp.clip(jnp.exp(math.log(2.0) - 1.3862944 * jax.random.uniform(streams_of[1], (IMAGES, C1), jnp.float32) ** shard_levels(streams_of[1], (IMAGES, C1), ((0, 8),), -0.2, 0.2)), 0.5, 2.0)
    bottom_cond = jnp.clip(jnp.exp(math.log(2.0) - 1.3862944 * jax.random.uniform(streams_of[2], (IMAGES, C2), jnp.float32) ** shard_levels(streams_of[2], (IMAGES, C2), ((0, 8),), -0.2, 0.2)), 0.5, 2.0)
    top_qkv = bell_draw(streams_of[3], (C1, 3 * C1), C1 ** -0.5, 0.25, ((0, 32),))
    top_scale = jnp.clip(jnp.exp(jax.random.uniform(streams_of[4], (C1 // HEAD,), jnp.float32, math.log(4.0), math.log(16.0))), 4.0, 16.0)
    merge_weight = bell_draw(streams_of[5], (4 * C1, C2), (4 * C1) ** -0.5, 0.125, ((0, 32),))
    bottom_qkv = bell_draw(streams_of[6], (C2, 3 * C2), C2 ** -0.5, 0.1875, ((0, 32),))
    bottom_scale = jnp.clip(jnp.exp(jax.random.uniform(streams_of[7], (C2 // HEAD,), jnp.float32, math.log(4.0), math.log(16.0))), 4.0, 16.0)
    out_cotangent = bell_draw(streams_of[8], (IMAGES, H2, W2, C2), 1.0, 6.0, ((0, 8), (1, 32)))
    return {"image_tokens": image_tokens, "top_cond": top_cond, "bottom_cond": bottom_cond, "top_qkv": top_qkv, "top_scale": top_scale, "merge_weight": merge_weight, "bottom_qkv": bottom_qkv, "bottom_scale": bottom_scale, "out_cotangent": out_cotangent}


epsilon = 1e-06

def rms_scale(values, gains):
    mean_sq = lax.optimization_barrier(jnp.mean(values * values, axis=-1, keepdims=True))
    return values * lax.rsqrt(mean_sq + epsilon) * gains

def head_norm(values, head_count):
    shaped = values.reshape(values.shape[:-1] + (head_count, values.shape[-1] // head_count))
    mean_sq = lax.optimization_barrier(jnp.mean(shaped * shaped, axis=-1, keepdims=True))
    return shaped * lax.rsqrt(mean_sq + epsilon)

def neighbour_attend(queries, keys, values, scales, first_row, grid_rows):
    query_rows, grid_cols, features = queries.shape
    head_count = scales.shape[0]
    head_size = features // head_count
    query_unit = head_norm(queries, head_count)
    key_unit = jnp.pad(head_norm(keys, head_count), ((0, 0), (3, 3), (0, 0), (0, 0)))
    value_heads = jnp.pad(values.reshape(keys.shape[0], grid_cols, head_count, head_size), ((0, 0), (3, 3), (0, 0), (0, 0)))
    row_pos = first_row + jnp.arange(query_rows, dtype=jnp.int32)
    col_pos = jnp.arange(grid_cols, dtype=jnp.int32)

    def one_row(carry, row_shift):
        numer, denom = carry
        key_rows = lax.dynamic_slice_in_dim(key_unit, row_shift, query_rows, 0)
        value_rows = lax.dynamic_slice_in_dim(value_heads, row_shift, query_rows, 0)
        key_row = row_pos + row_shift - 3
        row_ok = (key_row >= 0) & (key_row < grid_rows)
        for col_shift in range(7):
            key_part = key_rows[:, col_shift:col_shift + grid_cols]
            value_part = value_rows[:, col_shift:col_shift + grid_cols]
            key_col = col_pos + col_shift - 3
            col_ok = (key_col >= 0) & (key_col < grid_cols)
            inside = (row_ok[:, None] & col_ok[None, :]).astype(jnp.float32)
            score = scales * lax.optimization_barrier(jnp.mean(query_unit * key_part, axis=-1))
            weight = jnp.exp(score) * inside[:, :, None]
            numer = numer + weight[..., None] * value_part
            denom = denom + weight
        return ((numer, denom), None)
    start = (jnp.zeros(query_unit.shape, jnp.float32), jnp.zeros(query_unit.shape[:-1], jnp.float32))
    (numer, denom), _ = lax.scan(jax.checkpoint(one_row), start, jnp.arange(7, dtype=jnp.int32))
    return (numer / denom[..., None]).reshape(query_rows, grid_cols, features)

def global_attend(queries, keys, values, scales):
    depth = queries.shape[-1]
    query_unit = queries * lax.rsqrt(lax.optimization_barrier(jnp.mean(queries * queries, axis=-1, keepdims=True)) + epsilon)
    key_unit = keys * lax.rsqrt(lax.optimization_barrier(jnp.mean(keys * keys, axis=-1, keepdims=True)) + epsilon)
    score = jnp.einsum('qhd,khd->hqk', query_unit, key_unit) * (scales[:, None, None] / depth)
    weight = jnp.exp(score)
    probs = weight / lax.optimization_barrier(jnp.sum(weight, axis=-1, keepdims=True))
    return jnp.einsum('hqk,khd->qhd', probs, values)

def unshuffle(grid):
    grid_rows, grid_cols, features = grid.shape
    split = grid.reshape(grid_rows // 2, 2, grid_cols // 2, 2, features).transpose(0, 2, 1, 3, 4)
    return split.reshape(grid_rows // 2 * (grid_cols // 2), 4 * features)

def shuffle(flat, grid_rows, grid_cols, features):
    split = flat.reshape(grid_rows // 2, grid_cols // 2, 2, 2, features).transpose(0, 2, 1, 3, 4)
    return split.reshape(grid_rows, grid_cols, features)

def block_sum(left, right, block_count):
    left_blocks = left.reshape(block_count, -1, left.shape[-1])
    right_blocks = right.reshape(block_count, -1, right.shape[-1])

    def add_block(total, pair):
        product = jnp.dot(pair[0].T, pair[1], preferred_element_type=jnp.float32)
        rounded = lax.optimization_barrier(product.astype(jnp.bfloat16))
        return (total + rounded.astype(jnp.float32), None)
    start = jnp.zeros((left.shape[-1], right.shape[-1]), jnp.float32)
    total, _ = lax.scan(add_block, start, (left_blocks, right_blocks))
    return total

def reference(image_tokens, top_cond, bottom_cond, top_qkv, top_scale, merge_weight, bottom_qkv, bottom_scale, out_cotangent):
    grid_rows, grid_cols, top_width = image_tokens.shape[1:]
    low_width = bottom_qkv.shape[0]
    head_count = bottom_scale.shape[0]
    head_size = low_width // head_count
    low_rows = grid_rows // 2
    low_cols = grid_cols // 2
    seq_len = low_rows * low_cols

    def one_image(items):
        tokens, cond_top, cond_low, cotangent = items
        tokens_f = tokens.astype(jnp.float32)
        top_normed = rms_scale(tokens_f, cond_top).astype(jnp.bfloat16)
        top_flat = top_normed.reshape(grid_rows * grid_cols, top_width)
        top_proj = jnp.dot(top_flat, top_qkv, preferred_element_type=jnp.float32).astype(jnp.bfloat16)
        top_proj = top_proj.reshape(grid_rows, grid_cols, 3 * top_width)
        query_top = top_proj[..., :top_width].astype(jnp.float32)
        key_top = jnp.pad(top_proj[..., top_width:2 * top_width].astype(jnp.float32), ((3, 3), (0, 0), (0, 0)))
        value_top = jnp.pad(top_proj[..., 2 * top_width:].astype(jnp.float32), ((3, 3), (0, 0), (0, 0)))

        def attend_top(query_part, key_part, value_part):
            return neighbour_attend(query_part, key_part, value_part, top_scale, 0, grid_rows)
        top_out, top_pull = jax.vjp(attend_top, query_top, key_top, value_top)
        middle = (tokens_f + top_out).astype(jnp.bfloat16)
        unshuffled = unshuffle(middle)
        low = jnp.dot(unshuffled, merge_weight, preferred_element_type=jnp.float32).astype(jnp.bfloat16)
        low_f = low.astype(jnp.float32)
        low_normed = rms_scale(low_f, cond_low).astype(jnp.bfloat16)
        low_proj = jnp.dot(low_normed, bottom_qkv, preferred_element_type=jnp.float32).astype(jnp.bfloat16)
        grad_out = cotangent.reshape(seq_len, low_width)

        def by_head(block):
            return block.astype(jnp.float32).reshape(seq_len, head_count, head_size).transpose(1, 0, 2)[:, :, None, :]

        def one_head(parts):
            query_part, key_part, value_part, grad_part, scale_part = parts

            def attend_low(query_in, key_in, value_in):
                return global_attend(query_in, key_in, value_in, scale_part)
            attended, pull = jax.vjp(attend_low, query_part, key_part, value_part)
            grad_q, grad_k, grad_v = pull(grad_part)
            return (attended.astype(jnp.bfloat16), grad_q.astype(jnp.bfloat16), grad_k.astype(jnp.bfloat16), grad_v.astype(jnp.bfloat16))
        head_items = (by_head(low_proj[:, :low_width]), by_head(low_proj[:, low_width:2 * low_width]), by_head(low_proj[:, 2 * low_width:]), by_head(grad_out), bottom_scale[:, None])
        attended, grad_q, grad_k, grad_v = lax.map(one_head, head_items)

        def from_heads(block):
            return block[:, :, 0, :].transpose(1, 0, 2).reshape(seq_len, low_width)
        low_attention = from_heads(attended)
        output = (low_f + low_attention.astype(jnp.float32)).astype(jnp.bfloat16)
        grad_low_proj = jnp.concatenate([from_heads(grad_q), from_heads(grad_k), from_heads(grad_v)], axis=-1)
        back_low = jnp.dot(grad_low_proj, bottom_qkv.T, preferred_element_type=jnp.float32)
        _, pull_low = jax.vjp(lambda low_in: rms_scale(low_in, cond_low), low_f)
        grad_low = (grad_out.astype(jnp.float32) + pull_low(back_low)[0]).astype(jnp.bfloat16)
        back_merge = jnp.dot(grad_low, merge_weight.T, preferred_element_type=jnp.float32)
        grad_middle = shuffle(back_merge, grid_rows, grid_cols, top_width)
        grad_q1, grad_k1, grad_v1 = top_pull(grad_middle)
        grad_top_proj = jnp.concatenate([grad_q1, grad_k1[3:-3], grad_v1[3:-3]], axis=-1).astype(jnp.bfloat16)
        grad_top_flat = grad_top_proj.reshape(grid_rows * grid_cols, 3 * top_width)
        back_top = jnp.dot(grad_top_flat, top_qkv.T, preferred_element_type=jnp.float32).reshape(grid_rows, grid_cols, top_width)
        _, pull_top = jax.vjp(lambda top_in: rms_scale(top_in, cond_top), tokens_f)
        grad_tokens = (grad_middle + pull_top(back_top)[0]).astype(jnp.bfloat16)
        top_sum = block_sum(top_flat, grad_top_flat, N_ROWS)
        merge_sum = block_sum(unshuffled, grad_low, N_ROWS)
        low_sum = block_sum(low_normed, grad_low_proj, N_ROWS)
        return (output.reshape(low_rows, low_cols, low_width), grad_tokens, top_sum, merge_sum, low_sum)
    output, grad_tokens, top_sums, merge_sums, low_sums = lax.map(one_image, (image_tokens, top_cond, bottom_cond, out_cotangent))
    return (output, grad_tokens, lax.optimization_barrier(jnp.sum(top_sums, axis=0)), lax.optimization_barrier(jnp.sum(merge_sums, axis=0)), lax.optimization_barrier(jnp.sum(low_sums, axis=0)))
```

```python
import functools
import jax
import jax.numpy as jnp
from jax import lax
from jax.experimental import pallas as pl
from jax.experimental.pallas import tpu as pltpu
from jax.sharding import Mesh, PartitionSpec as P

epsilon = 1e-06
log2e = 1.4426950408889634
f32 = jnp.float32
bf16 = jnp.bfloat16
ROWS = ("x", "z")
DP = ("y", "c")
HEAD = 64
MIB = 1 << 20


def dot_nn(left, right):
    return jnp.dot(left, right, preferred_element_type=f32)


def dot_nt(left, right):
    return lax.dot_general(left, right, (((1,), (1,)), ((), ())), preferred_element_type=f32)


def dot_tn(left, right):
    return lax.dot_general(left, right, (((0,), (0,)), ((), ())), preferred_element_type=f32)


def unit_scale(x):
    return lax.rsqrt(jnp.mean(x * x, axis=-1, keepdims=True) + epsilon)


def unit_pull(x, scale, grad):
    inner = jnp.mean(x * grad, axis=-1, keepdims=True)
    return scale * grad - x * (scale * scale * scale * inner)


def grad_ext(grad, out):
    delta = jnp.sum(grad * out, axis=-1, keepdims=True)
    high = delta.astype(bf16).astype(f32)
    rest = delta - high
    lane = lax.broadcasted_iota(jnp.int32, grad.shape, 1)
    tail = jnp.where(lane == 0, -high, jnp.where(lane == 1, -rest, 0.0))
    return jnp.concatenate([grad, tail], axis=1).astype(bf16)


def vmem():
    return pl.BlockSpec(memory_space=pltpu.VMEM)


def smem():
    return pl.BlockSpec(memory_space=pltpu.SMEM)


def anywhere():
    return pl.BlockSpec(memory_space=pl.ANY)


def call(kernel, ins, outs, scratch=(), limit=40, flops=0, name=None):
    return pl.pallas_call(
        kernel,
        in_specs=ins,
        out_specs=[vmem() for _ in outs],
        out_shape=[jax.ShapeDtypeStruct(shape, kind) for shape, kind in outs],
        scratch_shapes=list(scratch),
        compiler_params=pltpu.CompilerParams(vmem_limit_bytes=limit * MIB),
        name=name,
    )


def neighbour_mask(first, grid_rows, cols, query_dim, shape):
    query = lax.broadcasted_iota(jnp.int32, shape, query_dim)
    key = lax.broadcasted_iota(jnp.int32, shape, 1 - query_dim)
    half = cols // 2

    def column(index):
        place = index % cols
        return 2 * (place % half) + place // half

    shift = key // cols - query // cols
    apart = column(key) - column(query)
    key_row = first - 3 + key // cols
    inside = (shift >= 0) & (shift <= 6) & (apart >= -3) & (apart <= 3)
    inside = inside & (key_row >= 0) & (key_row < grid_rows)
    return jnp.where(inside, 1.0, 0.0).astype(f32)


def project_top(pos_ref, flat_ref, own_ref, other_ref, proj_ref, up_ref, down_ref):
    core = pos_ref[1]
    width = own_ref.shape[1]
    tokens, edge = flat_ref.shape[0], up_ref.shape[0]
    here = pl.multiple_of(core * width, 128)
    there = pl.multiple_of((1 - core) * width, 128)
    proj_ref[:, pl.ds(here, width)] = dot_nn(flat_ref[...], own_ref[...]).astype(bf16)
    proj_ref[:, pl.ds(there, width)] = dot_nn(flat_ref[...], other_ref[...]).astype(bf16)
    top = flat_ref.shape[1]
    up_ref[...] = proj_ref[0:edge, top:]
    down_ref[...] = proj_ref[tokens - edge :, top:]


def head_parts(proj_ref, lo_ref, hi_ref, at, top):
    key = jnp.concatenate(
        [
            lo_ref[:, at : at + HEAD],
            proj_ref[:, top + at : top + at + HEAD],
            hi_ref[:, at : at + HEAD],
        ],
        axis=0,
    ).astype(f32)
    value = jnp.concatenate(
        [
            lo_ref[:, top + at : top + at + HEAD],
            proj_ref[:, 2 * top + at : 2 * top + at + HEAD],
            hi_ref[:, top + at : top + at + HEAD],
        ],
        axis=0,
    )
    query = proj_ref[:, at : at + HEAD].astype(f32)
    return query, key, value


def top_forward(
    grid_rows, cols, pos_ref, scale_ref, tok_ref, proj_ref, lo_ref, hi_ref,
    unsh_ref, out_ref, inv_ref, mask_ref,
):
    top = tok_ref.shape[1]
    mask_ref[...] = neighbour_mask(pos_ref[0], grid_rows, cols, 0, mask_ref.shape)
    for pair in range(top // (2 * HEAD)):
        outs, invs = [], []
        for head in (2 * pair, 2 * pair + 1):
            query, key, value = head_parts(proj_ref, lo_ref, hi_ref, head * HEAD, top)
            gain = scale_ref[head] * (log2e / HEAD)
            query = (query * (unit_scale(query) * gain)).astype(bf16)
            key = (key * unit_scale(key)).astype(bf16)
            wide = jnp.concatenate([value, jnp.ones_like(value)], axis=1)
            weight = (jnp.exp2(dot_nt(query, key)) * mask_ref[...]).astype(bf16)
            both = dot_nn(weight, wide)
            inverse = 1.0 / both[:, HEAD:]
            outs.append(both[:, :HEAD] * inverse)
            invs.append(inverse)
        at = pair * 2 * HEAD
        out_ref[:, at : at + 2 * HEAD] = jnp.concatenate(outs, axis=1)
        inv_ref[:, at : at + 2 * HEAD] = jnp.concatenate(invs, axis=1)
    half = cols // 2
    for row in range(tok_ref.shape[0] // cols):
        for odd in range(2):
            at = row * cols + odd * half
            part = tok_ref[at : at + half, :].astype(f32) + out_ref[at : at + half, :]
            low_at = (row // 2) * half
            place = (2 * (row % 2) + odd) * top
            unsh_ref[low_at : low_at + half, place : place + top] = part.astype(bf16)


def top_backward(
    grid_rows, cols, pos_ref, scale_ref, proj_ref, lo_ref, hi_ref, out_ref, inv_ref, grad_ref,
    gq_ref, gmid_ref, gup_ref, gdown_ref, mask_ref,
):
    tokens, top = out_ref.shape
    edge = lo_ref.shape[0]
    mask_ref[...] = neighbour_mask(pos_ref[0], grid_rows, cols, 1, mask_ref.shape)
    for pair in range(top // (2 * HEAD)):
        gqs, gks, gvs = [], [], []
        for head in (2 * pair, 2 * pair + 1):
            at = head * HEAD
            query, key, value = head_parts(proj_ref, lo_ref, hi_ref, at, top)
            gain = scale_ref[head] * (1.0 / HEAD)
            query_scale = unit_scale(query)
            key_scale = unit_scale(key)
            query_unit = (query * (query_scale * (gain * log2e))).astype(bf16)
            key_f = key * key_scale
            key_unit = key_f.astype(bf16)
            key_t = jnp.concatenate([key_f, jnp.zeros_like(key_f)], axis=1).T.astype(bf16)
            wide = jnp.concatenate([value, jnp.ones_like(value)], axis=1)
            grad = grad_ref[:, at : at + HEAD] * inv_ref[:, at : at + HEAD]
            grad = grad_ext(grad, out_ref[:, at : at + HEAD])
            weight = jnp.exp2(dot_nt(key_unit, query_unit)) * mask_ref[...]
            slope = (weight * dot_nt(wide, grad)).astype(bf16)
            gvs.append(dot_nn(weight.astype(bf16), grad)[:, :HEAD])
            gk = dot_nn(slope, query_unit) * (1.0 / log2e)
            gks.append(unit_pull(key, key_scale, gk))
            gq = dot_nn(key_t, slope).T[:, :HEAD] * gain
            gqs.append(unit_pull(query, query_scale, gq))
        at = pair * 2 * HEAD
        gq_ref[:, at : at + 2 * HEAD] = jnp.concatenate(gqs, axis=1).astype(bf16)
        for base, parts in ((at, gks), (top + at, gvs)):
            whole = jnp.concatenate(parts, axis=1)
            gup_ref[:, base : base + 2 * HEAD] = whole[:edge].astype(bf16)
            gmid_ref[:, base : base + 2 * HEAD] = whole[edge : edge + tokens]
            gdown_ref[:, base : base + 2 * HEAD] = whole[edge + tokens :].astype(bf16)


def weight_copies(core, own_ref, other_ref, merge_buf, low_buf, sems):
    merge_rows = merge_buf.shape[1]
    low_rows = low_buf.shape[2]
    half = own_ref.shape[2]
    here = pl.multiple_of(core * half, 128)
    there = pl.multiple_of((1 - core) * half, 128)
    merge, low = [], []
    for side, (ref, place) in enumerate(((own_ref, here), (other_ref, there))):
        merge.append(
            pltpu.make_async_copy(
                ref.at[:, 0:merge_rows, :],
                merge_buf.at[:, :, pl.ds(place, half)],
                sems.at[4 * side],
            )
        )
    for block in range(3):
        at = merge_rows + block * low_rows
        for side, (ref, place) in enumerate(((own_ref, here), (other_ref, there))):
            low.append(
                pltpu.make_async_copy(
                    ref.at[:, at : at + low_rows, :],
                    low_buf.at[block, :, :, pl.ds(place, half)],
                    sems.at[4 * side + 1 + block],
                )
            )
    return merge, low


def flat(ref_value):
    return ref_value.reshape(ref_value.shape[0] * ref_value.shape[1], ref_value.shape[2])


def low_forward(
    pos_ref, unsh_ref, cond_ref, cot_ref, own_ref, other_ref,
    low_ref, normed_ref, send_ref, merge_buf, low_buf, sems,
):
    merge, lower = weight_copies(pos_ref[1], own_ref, other_ref, merge_buf, low_buf, sems)
    for copy in merge + lower:
        copy.start()
    for copy in merge:
        copy.wait()
    low = dot_nn(unsh_ref[...], flat(merge_buf[...])).astype(bf16)
    low_ref[...] = low
    low = low.astype(f32)
    normed = (low * unit_scale(low) * cond_ref[...]).astype(bf16)
    normed_ref[...] = normed
    parts = []
    for block in range(3):
        lower[2 * block].wait()
        lower[2 * block + 1].wait()
        parts.append(dot_nn(normed, flat(low_buf[block])).astype(bf16))
    query, key, value = parts
    cot = cot_ref[...]
    tokens = query.shape[0]
    share = tokens // 2
    for head in range(query.shape[1] // HEAD):
        at = head * HEAD
        key_value = jnp.concatenate([key[:, at : at + HEAD], value[:, at : at + HEAD]], axis=1)
        query_grad = jnp.concatenate([query[:, at : at + HEAD], cot[:, at : at + HEAD]], axis=1)
        for part in range(2):
            send_ref[2 * head + part, 0:tokens, :] = key_value
            send_ref[2 * head + part, tokens:, :] = query_grad[part * share : (part + 1) * share]


def low_attend(pos_ref, scale_ref, recv_ref, back_ref, key_s, key_t_s, wide_s, wide_t_s, gk_s, gv_s):
    gain = scale_ref[pos_ref[2]] * (1.0 / HEAD)
    sources = recv_ref.shape[0]
    tokens = recv_ref.shape[1] * 2 // 3
    share = tokens // 2
    keys = sources * tokens
    both = recv_ref[:, 0:tokens, :].reshape(keys, 2 * HEAD)
    key = both[:, :HEAD].astype(f32)
    key_scale = unit_scale(key)
    key_f = key * key_scale
    key_s[...] = key_f.astype(bf16)
    key_t_s[...] = jnp.concatenate([key_f, jnp.zeros_like(key_f)], axis=1).T.astype(bf16)
    wide = jnp.concatenate([both[:, HEAD:].astype(f32), jnp.ones_like(key_f)], axis=1)
    wide_s[...] = wide.astype(bf16)
    wide_t_s[...] = wide.T.astype(bf16)
    group = 8
    rows = group * share
    for block in range(sources // group):
        item = recv_ref[block * group : (block + 1) * group, tokens:, :].reshape(rows, 2 * HEAD)
        item = item.astype(f32)
        query, cot = item[:, :HEAD], item[:, HEAD:]
        query_scale = unit_scale(query)
        query_unit = (query * (query_scale * (gain * log2e))).astype(bf16)
        weight = jnp.exp2(dot_nt(key_s[...], query_unit)).astype(bf16)
        total = dot_nn(wide_t_s[...], weight).T
        inverse = 1.0 / total[:, HEAD:]
        out = total[:, :HEAD] * inverse
        grad = grad_ext(cot * inverse, out)
        slope = (weight.astype(f32) * dot_nt(wide_s[...], grad)).astype(bf16)
        gv = dot_nn(weight, grad)
        gk = dot_nn(slope, query_unit)
        if block == 0:
            gv_s[...] = gv
            gk_s[...] = gk
        else:
            gv_s[...] += gv
            gk_s[...] += gk
        gq = dot_nn(key_t_s[...], slope).T[:, :HEAD] * gain
        gq = unit_pull(query, query_scale, gq)
        result = jnp.concatenate([out, gq], axis=1).astype(bf16)
        back_ref[block * group : (block + 1) * group, tokens:, :] = result.reshape(
            group, share, 2 * HEAD
        )
    gk = unit_pull(key, key_scale, gk_s[...] * (1.0 / log2e))
    result = jnp.concatenate([gk, gv_s[:, :HEAD]], axis=1).astype(bf16)
    back_ref[:, 0:tokens, :] = result.reshape(sources, tokens, 2 * HEAD)


def low_backward(
    pos_ref, ret_ref, low_ref, cond_ref, cot_ref, own_ref, other_ref,
    output_ref, glp_ref, glow_ref, gmid_ref, proj_s, merge_buf, low_buf, sems,
):
    merge, lower = weight_copies(pos_ref[1], own_ref, other_ref, merge_buf, low_buf, sems)
    for copy in lower + merge:
        copy.start()
    tokens, width = low_ref.shape
    share = tokens // 2
    low = low_ref[...].astype(f32)
    for pair in range(width // (2 * HEAD)):
        outs, gqs, gks, gvs = [], [], [], []
        for head in (2 * pair, 2 * pair + 1):
            first, second = ret_ref[2 * head], ret_ref[2 * head + 1]
            sums = first[:tokens].astype(f32) + second[:tokens].astype(f32)
            gks.append(sums[:, :HEAD])
            gvs.append(sums[:, HEAD:])
            query = jnp.concatenate([first[tokens:], second[tokens:]], axis=0)
            outs.append(query[:, :HEAD])
            gqs.append(query[:, HEAD:])
        at = pair * 2 * HEAD
        out = jnp.concatenate(outs, axis=1).astype(f32)
        output_ref[:, at : at + 2 * HEAD] = (low[:, at : at + 2 * HEAD] + out).astype(bf16)
        proj_s[:, at : at + 2 * HEAD] = jnp.concatenate(gqs, axis=1)
        proj_s[:, width + at : width + at + 2 * HEAD] = jnp.concatenate(gks, axis=1).astype(bf16)
        proj_s[:, 2 * width + at : 2 * width + at + 2 * HEAD] = jnp.concatenate(
            gvs, axis=1
        ).astype(bf16)
    groups, _, share_cols = glp_ref.shape
    for part in range(groups):
        glp_ref[part] = proj_s[:, part * share_cols : (part + 1) * share_cols]
    back = jnp.zeros((tokens, width), f32)
    for block in range(3):
        lower[2 * block].wait()
        lower[2 * block + 1].wait()
        back = back + dot_nt(proj_s[:, block * width : (block + 1) * width], flat(low_buf[block]))
    grad = unit_pull(low, unit_scale(low), back * cond_ref[...])
    grad = (cot_ref[...].astype(f32) + grad).astype(bf16)
    share_cols = glow_ref.shape[2]
    for part in range(groups):
        glow_ref[part] = grad[:, part * share_cols : (part + 1) * share_cols]
    for copy in merge:
        copy.wait()
    wide = dot_nt(grad, flat(merge_buf[...]))
    top = gmid_ref.shape[1]
    half = 16
    for row in range(2 * tokens // half):
        for odd in range(2):
            at = (2 * row + odd) * half
            low_at = (row // 2) * half
            place = (2 * (row % 2) + odd) * top
            gmid_ref[at : at + half, :] = wide[low_at : low_at + half, place : place + top]


def gather_top_grads(gq_ref, gmid_ref, prev_ref, next_ref, whole_ref, parts_ref):
    tokens, top = gq_ref.shape
    edge = prev_ref.shape[0]
    whole_ref[:, :top] = gq_ref[...]
    whole_ref[0:edge, top:] = (gmid_ref[0:edge] + prev_ref[...].astype(f32)).astype(bf16)
    whole_ref[edge : tokens - edge, top:] = gmid_ref[edge : tokens - edge].astype(bf16)
    whole_ref[tokens - edge :, top:] = (
        gmid_ref[tokens - edge :] + next_ref[...].astype(f32)
    ).astype(bf16)
    groups, _, cols = parts_ref.shape
    for part in range(groups):
        parts_ref[part] = whole_ref[:, part * cols : (part + 1) * cols]


def finish_tokens(pos_ref, whole_ref, tok_ref, cond_ref, grad_ref, own_ref, other_ref, out_ref):
    core = pos_ref[1]
    width = own_ref.shape[1]
    here = pl.multiple_of(core * width, 128)
    there = pl.multiple_of((1 - core) * width, 128)
    back = dot_nt(whole_ref[:, pl.ds(here, width)], own_ref[...])
    back = back + dot_nt(whole_ref[:, pl.ds(there, width)], other_ref[...])
    tok = tok_ref[...].astype(f32)
    out_ref[...] = (
        grad_ref[...] + unit_pull(tok, unit_scale(tok), back * cond_ref[...])
    ).astype(bf16)


def to_all(block, axis):
    return lax.all_to_all(block, axis, split_axis=0, concat_axis=0, tiled=True)


def spread(block, axis):
    count = lax.axis_size(axis)
    return lax.all_to_all(
        jnp.broadcast_to(block[None], (count,) + block.shape), axis, split_axis=0, concat_axis=0
    )


def swap_cores(block):
    return lax.ppermute(block, "c", [(0, 1), (1, 0)])


def body(
    image_tokens,
    top_cond,
    bottom_cond,
    top_qkv,
    top_scale,
    merge_weight,
    bottom_qkv,
    bottom_scale,
    out_cotangent,
):
    _, shard_rows, cols, top = image_tokens.shape
    width = bottom_cond.shape[1]
    row_devices = lax.axis_size(ROWS)
    images = lax.axis_size(DP)
    grid_rows = shard_rows * row_devices
    tokens = shard_rows * cols
    low_tokens = tokens // 4
    edge = 3 * cols
    row_at = lax.axis_index(ROWS)
    core = lax.axis_index("c")
    pos = jnp.stack([row_at * shard_rows, core, row_at // 2]).astype(jnp.int32)

    low_rows = bottom_qkv.shape[0]
    merge_rows = merge_weight.shape[0]
    pack_rows = merge_rows + 3 * low_rows
    packed = jnp.concatenate(
        [merge_weight] + [bottom_qkv[:, i * width : (i + 1) * width] for i in range(3)], axis=0
    )
    packed = lax.dynamic_slice_in_dim(packed, core * (width // 2), width // 2, 1)
    w_own = lax.all_gather(packed, ROWS, axis=0, tiled=False)
    w_other = swap_cores(w_own)
    top_half = top_qkv.shape[1] // 2
    top_piece = lax.dynamic_slice_in_dim(top_qkv, core * top_half, top_half, 1)
    top_own = spread(spread(top_piece, "z"), "x").reshape(top, top_half)
    top_other = swap_cores(top_own)

    tok = image_tokens[0].reshape(shard_rows, cols // 2, 2, top).transpose(0, 2, 1, 3)
    tok = tok.reshape(tokens, top)
    tok_f = tok.astype(f32)
    top_flat = (tok_f * unit_scale(tok_f) * top_cond[0]).astype(bf16)
    proj, up, down = call(
        project_top,
        [smem(), vmem(), vmem(), vmem()],
        [((tokens, 3 * top), bf16), ((edge, 2 * top), bf16), ((edge, 2 * top), bf16)],
        name="project_top",
    )(pos, top_flat, top_own, top_other)
    forward = [(i, i + 1) for i in range(row_devices - 1)]
    backward = [(i + 1, i) for i in range(row_devices - 1)]
    lo = lax.ppermute(down, ROWS, forward)
    hi = lax.ppermute(up, ROWS, backward)
    unshuffled, top_out, top_inv = call(
        functools.partial(top_forward, grid_rows, cols),
        [smem(), smem()] + [vmem()] * 4,
        [((low_tokens, 4 * top), bf16), ((tokens, top), f32), ((tokens, top), f32)],
        [pltpu.VMEM((tokens, tokens + 2 * edge), f32)],
        name="top_forward",
    )(pos, top_scale, tok, proj, lo, hi)

    cot = out_cotangent[0].reshape(low_tokens, width)
    weight_scratch = [
        pltpu.VMEM((row_devices, merge_rows, width), bf16),
        pltpu.VMEM((3, row_devices, low_rows, width), bf16),
        pltpu.SemaphoreType.DMA((8,)),
    ]
    exchange = (row_devices, low_tokens * 3 // 2, 2 * HEAD)
    low, low_normed, send = call(
        low_forward,
        [smem()] + [vmem()] * 3 + [anywhere()] * 2,
        [((low_tokens, width), bf16), ((low_tokens, width), bf16), (exchange, bf16)],
        weight_scratch,
        name="low_forward",
    )(pos, unshuffled, bottom_cond, cot, w_own, w_other)
    recv = to_all(send, ROWS)
    keys = row_devices * low_tokens
    (back,) = call(
        low_attend,
        [smem(), smem(), vmem()],
        [(exchange, bf16)],
        [
            pltpu.VMEM((keys, HEAD), bf16),
            pltpu.VMEM((2 * HEAD, keys), bf16),
            pltpu.VMEM((keys, 2 * HEAD), bf16),
            pltpu.VMEM((2 * HEAD, keys), bf16),
            pltpu.VMEM((keys, HEAD), f32),
            pltpu.VMEM((keys, 2 * HEAD), f32),
        ],
        name="low_attend",
    )(pos, bottom_scale, recv)
    ret = to_all(back, ROWS)
    output, grad_proj, grad_low, grad_middle = call(
        low_backward,
        [smem()] + [vmem()] * 4 + [anywhere()] * 2,
        [
            ((low_tokens, width), bf16),
            ((images, low_tokens, 3 * width // images), bf16),
            ((images, low_tokens, width // images), bf16),
            ((tokens, top), f32),
        ],
        [pltpu.VMEM((low_tokens, 3 * width), bf16)] + weight_scratch,
        name="low_backward",
    )(pos, ret, low, bottom_cond, cot, w_own, w_other)

    gq, gmid, gup, gdown = call(
        functools.partial(top_backward, grid_rows, cols),
        [smem(), smem()] + [vmem()] * 6,
        [
            ((tokens, top), bf16),
            ((tokens, 2 * top), f32),
            ((edge, 2 * top), bf16),
            ((edge, 2 * top), bf16),
        ],
        [pltpu.VMEM((tokens + 2 * edge, tokens), f32)],
        name="top_backward",
    )(pos, top_scale, proj, lo, hi, top_out, top_inv, grad_middle)
    from_next = lax.ppermute(gup, ROWS, backward)
    from_prev = lax.ppermute(gdown, ROWS, forward)
    grad_top, grad_top_parts = call(
        gather_top_grads,
        [vmem()] * 4,
        [((tokens, 3 * top), bf16), ((images, tokens, 3 * top // images), bf16)],
        name="gather_top_grads",
    )(gq, gmid, from_prev, from_next)
    (grad_tokens,) = call(
        finish_tokens,
        [smem()] + [vmem()] * 6,
        [((tokens, top), bf16)],
        name="finish_tokens",
    )(pos, grad_top, tok, top_cond, grad_middle, top_own, top_other)

    top_flat_late, _ = lax.optimization_barrier((top_flat, w_own))
    top_all = lax.all_gather(top_flat_late, DP, axis=0, tiled=True)
    unsh_all = lax.all_gather(unshuffled, DP, axis=0, tiled=True)
    normed_all = lax.all_gather(low_normed, DP, axis=0, tiled=True)
    proj_all = to_all(grad_proj, DP).reshape(images * low_tokens, 3 * width // images)
    glow_all = to_all(grad_low, DP).reshape(images * low_tokens, width // images)
    part_low = dot_tn(normed_all, proj_all).astype(bf16)
    part_merge = dot_tn(unsh_all, glow_all).astype(bf16)
    pieces = part_low.shape[1] // 128
    part_low = part_low.reshape(row_devices, low_rows, pieces, 128).transpose(0, 2, 1, 3)
    part_low = part_low.reshape(row_devices, pieces * low_rows, 128)
    part_merge = part_merge.reshape(row_devices, merge_rows, 128)
    sums = to_all(jnp.concatenate([part_merge, part_low], axis=1), ROWS)
    sums = jnp.sum(sums.astype(f32), axis=0)
    sum_merge = sums[:merge_rows]
    sum_low = sums[merge_rows:].reshape(pieces, low_rows, 128).transpose(1, 0, 2)
    sum_low = sum_low.reshape(low_rows, pieces * 128)
    top_cols = 3 * top // images
    parts_all = to_all(grad_top_parts, DP).reshape(images * tokens, top_cols)
    part_top = dot_tn(top_all, parts_all).astype(bf16)
    part_top = to_all(part_top.reshape(row_devices, top // row_devices, top_cols), ROWS)
    sum_top = jnp.sum(part_top.astype(f32), axis=0)

    grad_tokens = grad_tokens.reshape(shard_rows, 2, cols // 2, top).transpose(0, 2, 1, 3)
    return (
        output.reshape(1, shard_rows // 2, cols // 2, width),
        grad_tokens.reshape(1, shard_rows, cols, top),
        sum_top,
        sum_merge,
        sum_low,
    )


def solution(mesh):
    images, row_devices = mesh.shape["dp"], mesh.shape["rows"]
    grid = mesh.devices.reshape(images // 2, 2, row_devices // 8, 8)
    split = Mesh(grid, ("y", "c", "x", "z"))
    placed = (
        P(DP, ROWS, None, None),
        P(DP, None),
        P(DP, None),
        P(ROWS, None),
        P(),
        P(ROWS, None),
        P(ROWS, None),
        P(),
        P(DP, ROWS, None, None),
    )
    return jax.shard_map(
        body,
        mesh=split,
        in_specs=placed,
        out_specs=(
            P(DP, ROWS, None, None),
            P(DP, ROWS, None, None),
            P(ROWS, DP),
            P(ROWS, DP),
            P(ROWS, DP),
        ),
        check_vma=False,
    )
```

```python
import functools
import jax
import jax.numpy as jnp
from jax import lax
from jax.experimental import pallas as pl
from jax.experimental.pallas import tpu as pltpu
from jax.sharding import Mesh, PartitionSpec as P

epsilon = 1e-06
log2e = 1.4426950408889634
f32 = jnp.float32
bf16 = jnp.bfloat16
ROWS = ("x", "z")
DP = ("y", "c")
HEAD = 64
MIB = 1 << 20


def dot_nn(left, right):
    return jnp.dot(left, right, preferred_element_type=f32)


def dot_nt(left, right):
    return lax.dot_general(left, right, (((1,), (1,)), ((), ())), preferred_element_type=f32)


def dot_tn(left, right):
    return lax.dot_general(left, right, (((0,), (0,)), ((), ())), preferred_element_type=f32)


def unit_scale(x):
    return lax.rsqrt(jnp.mean(x * x, axis=-1, keepdims=True) + epsilon)


def unit_pull(x, scale, grad):
    inner = jnp.mean(x * grad, axis=-1, keepdims=True)
    return scale * grad - x * (scale * scale * scale * inner)


def grad_ext(grad, out):
    delta = jnp.sum(grad * out, axis=-1, keepdims=True)
    high = delta.astype(bf16).astype(f32)
    rest = delta - high
    lane = lax.broadcasted_iota(jnp.int32, grad.shape, 1)
    tail = jnp.where(lane == 0, -high, jnp.where(lane == 1, -rest, 0.0))
    return jnp.concatenate([grad, tail], axis=1).astype(bf16)


def vmem():
    return pl.BlockSpec(memory_space=pltpu.VMEM)


def smem():
    return pl.BlockSpec(memory_space=pltpu.SMEM)


def anywhere():
    return pl.BlockSpec(memory_space=pl.ANY)


def call(kernel, ins, outs, scratch=(), limit=40, micros=2, name=None):
    return pl.pallas_call(
        kernel,
        in_specs=ins,
        out_specs=[vmem() for _ in outs],
        out_shape=[jax.ShapeDtypeStruct(shape, kind) for shape, kind in outs],
        scratch_shapes=list(scratch),
        compiler_params=pltpu.CompilerParams(vmem_limit_bytes=limit * MIB),
        cost_estimate=pl.CostEstimate(
            flops=micros * 1000000000, bytes_accessed=micros * 3000000, transcendentals=0
        ),
        name=name,
    )


def neighbour_mask(first, grid_rows, cols, query_dim, shape):
    query = lax.broadcasted_iota(jnp.int32, shape, query_dim)
    key = lax.broadcasted_iota(jnp.int32, shape, 1 - query_dim)
    half = cols // 2

    def column(index):
        place = index % cols
        return 2 * (place % half) + place // half

    shift = key // cols - query // cols
    apart = column(key) - column(query)
    key_row = first - 3 + key // cols
    inside = (shift >= 0) & (shift <= 6) & (apart >= -3) & (apart <= 3)
    inside = inside & (key_row >= 0) & (key_row < grid_rows)
    return jnp.where(inside, 1.0, 0.0).astype(f32)


def head_parts(proj_ref, at, top, tokens):
    edge = (proj_ref.shape[0] - tokens) // 2
    query = proj_ref[edge : edge + tokens, at : at + HEAD].astype(f32)
    key = proj_ref[:, top + at : top + at + HEAD].astype(f32)
    value = proj_ref[:, 2 * top + at : 2 * top + at + HEAD]
    return query, key, value


def top_forward(
    grid_rows, cols, pos_ref, scale_ref, tok_ref, flat_ref, lo_ref, hi_ref, own_ref, other_ref,
    unsh_ref, out_ref, inv_ref, proj_ref, mask_ref,
):
    tokens, top = tok_ref.shape
    core = pos_ref[1]
    width = own_ref.shape[1]
    ext = jnp.concatenate([lo_ref[...], flat_ref[...], hi_ref[...]], axis=0)
    here = pl.multiple_of(core * width, 128)
    there = pl.multiple_of((1 - core) * width, 128)
    proj_ref[:, pl.ds(here, width)] = dot_nn(ext, own_ref[...]).astype(bf16)
    proj_ref[:, pl.ds(there, width)] = dot_nn(ext, other_ref[...]).astype(bf16)
    mask_ref[...] = neighbour_mask(pos_ref[0], grid_rows, cols, 0, mask_ref.shape)
    for pair in range(top // (2 * HEAD)):
        outs, invs = [], []
        for head in (2 * pair, 2 * pair + 1):
            query, key, value = head_parts(proj_ref, head * HEAD, top, tokens)
            gain = scale_ref[head] * (log2e / HEAD)
            query = (query * (unit_scale(query) * gain)).astype(bf16)
            key = (key * unit_scale(key)).astype(bf16)
            wide = jnp.concatenate([value, jnp.ones_like(value)], axis=1)
            weight = (jnp.exp2(dot_nt(query, key)) * mask_ref[...]).astype(bf16)
            both = dot_nn(weight, wide)
            inverse = 1.0 / both[:, HEAD:]
            outs.append(both[:, :HEAD] * inverse)
            invs.append(inverse)
        at = pair * 2 * HEAD
        out_ref[:, at : at + 2 * HEAD] = jnp.concatenate(outs, axis=1)
        inv_ref[:, at : at + 2 * HEAD] = jnp.concatenate(invs, axis=1)
    half = cols // 2
    for row in range(tok_ref.shape[0] // cols):
        for odd in range(2):
            at = row * cols + odd * half
            part = tok_ref[at : at + half, :].astype(f32) + out_ref[at : at + half, :]
            low_at = (row // 2) * half
            place = (2 * (row % 2) + odd) * top
            unsh_ref[low_at : low_at + half, place : place + top] = part.astype(bf16)


def top_backward(
    grid_rows, cols, pos_ref, scale_ref, proj_ref, out_ref, inv_ref, grad_ref,
    gq_ref, gmid_ref, gup_ref, gdown_ref, mask_ref,
):
    tokens, top = out_ref.shape
    edge = gup_ref.shape[0]
    mask_ref[...] = neighbour_mask(pos_ref[0], grid_rows, cols, 1, mask_ref.shape)
    for pair in range(top // (2 * HEAD)):
        gqs, gks, gvs = [], [], []
        for head in (2 * pair, 2 * pair + 1):
            at = head * HEAD
            query, key, value = head_parts(proj_ref, at, top, tokens)
            gain = scale_ref[head] * (1.0 / HEAD)
            query_scale = unit_scale(query)
            key_scale = unit_scale(key)
            query_unit = (query * (query_scale * (gain * log2e))).astype(bf16)
            key_f = key * key_scale
            key_unit = key_f.astype(bf16)
            key_t = jnp.concatenate([key_f, jnp.zeros_like(key_f)], axis=1).T.astype(bf16)
            wide = jnp.concatenate([value, jnp.ones_like(value)], axis=1)
            grad = grad_ref[:, at : at + HEAD] * inv_ref[:, at : at + HEAD]
            grad = grad_ext(grad, out_ref[:, at : at + HEAD])
            weight = jnp.exp2(dot_nt(key_unit, query_unit)) * mask_ref[...]
            slope = (weight * dot_nt(wide, grad)).astype(bf16)
            gvs.append(dot_nn(weight.astype(bf16), grad)[:, :HEAD])
            gk = dot_nn(slope, query_unit) * (1.0 / log2e)
            gks.append(unit_pull(key, key_scale, gk))
            gq = dot_nn(key_t, slope).T[:, :HEAD] * gain
            gqs.append(unit_pull(query, query_scale, gq))
        at = pair * 2 * HEAD
        gq_ref[:, at : at + 2 * HEAD] = jnp.concatenate(gqs, axis=1).astype(bf16)
        for base, parts in ((at, gks), (top + at, gvs)):
            whole = jnp.concatenate(parts, axis=1)
            gup_ref[:, base : base + 2 * HEAD] = whole[:edge].astype(bf16)
            gmid_ref[:, base : base + 2 * HEAD] = whole[edge : edge + tokens]
            gdown_ref[:, base : base + 2 * HEAD] = whole[edge + tokens :].astype(bf16)


def weight_copies(pos_ref, weights, merge_buf, low_buf, sems):
    steps, rows = merge_buf.shape[1], merge_buf.shape[3]
    merge, low = [[], []], [[], []]
    for side in range(2):
        for step in range(steps):
            place = lax.rem(pos_ref[3] + steps - step, steps)
            merge[side].append(
                pltpu.make_async_copy(
                    weights[side].at[:, step, 0:rows, :],
                    merge_buf.at[side, place],
                    sems.at[side, step],
                )
            )
            low[side].append(
                pltpu.make_async_copy(
                    weights[side].at[:, step, rows:, :],
                    low_buf.at[side, place],
                    sems.at[side, steps + step],
                )
            )
    return merge, low


def merge_block(merge_buf, side):
    part = merge_buf[side]
    return part.reshape(part.shape[0] * part.shape[1] * part.shape[2], part.shape[3])


def low_block(low_buf, side, block):
    rows = low_buf.shape[3] // 3
    part = low_buf[side, :, :, block * rows : (block + 1) * rows, :]
    return part.reshape(part.shape[0] * part.shape[1] * rows, part.shape[3])


def low_forward(pos_ref, unsh_ref, cond_ref, cot_ref, *refs):
    weights, (low_ref, normed_ref, send_ref, proj_s, merge_buf, low_buf, sems) = refs[:-7], refs[-7:]
    merge, lower = weight_copies(pos_ref, weights, merge_buf, low_buf, sems)
    for copy in merge[0] + merge[1] + lower[0] + lower[1]:
        copy.start()
    half = merge_buf.shape[4]
    width = 2 * half
    core = pos_ref[1]
    places = [core * half, (1 - core) * half]
    for side in range(2):
        for copy in merge[side]:
            copy.wait()
        place = pl.multiple_of(places[side], 128)
        low_ref[:, pl.ds(place, half)] = dot_nn(
            unsh_ref[...], merge_block(merge_buf, side)
        ).astype(bf16)
    low = low_ref[...].astype(f32)
    normed = (low * unit_scale(low) * cond_ref[...]).astype(bf16)
    normed_ref[...] = normed
    for side in range(2):
        for copy in lower[side]:
            copy.wait()
        for block in range(3):
            place = pl.multiple_of(block * width + places[side], 128)
            proj_s[:, pl.ds(place, half)] = dot_nn(
                normed, low_block(low_buf, side, block)
            ).astype(bf16)
    query, key, value = (proj_s[:, i * width : (i + 1) * width] for i in range(3))
    cot = cot_ref[...]
    tokens = query.shape[0]
    share = tokens // 2
    for head in range(query.shape[1] // HEAD):
        at = head * HEAD
        key_value = jnp.concatenate([key[:, at : at + HEAD], value[:, at : at + HEAD]], axis=1)
        query_grad = jnp.concatenate([query[:, at : at + HEAD], cot[:, at : at + HEAD]], axis=1)
        for part in range(2):
            send_ref[2 * head + part, 0:tokens, :] = key_value
            send_ref[2 * head + part, tokens:, :] = query_grad[part * share : (part + 1) * share]


def low_attend(pos_ref, scale_ref, recv_ref, back_ref, key_s, key_t_s, wide_s, wide_t_s, gk_s, gv_s):
    gain = scale_ref[pos_ref[2]] * (1.0 / HEAD)
    sources = recv_ref.shape[0]
    tokens = recv_ref.shape[1] * 2 // 3
    share = tokens // 2
    keys = sources * tokens
    both = recv_ref[:, 0:tokens, :].reshape(keys, 2 * HEAD)
    key = both[:, :HEAD].astype(f32)
    key_scale = unit_scale(key)
    key_f = key * key_scale
    key_s[...] = key_f.astype(bf16)
    key_t_s[...] = jnp.concatenate([key_f, jnp.zeros_like(key_f)], axis=1).T.astype(bf16)
    wide = jnp.concatenate([both[:, HEAD:].astype(f32), jnp.ones_like(key_f)], axis=1)
    wide_s[...] = wide.astype(bf16)
    wide_t_s[...] = wide.T.astype(bf16)
    group = 8
    rows = group * share
    for block in range(sources // group):
        item = recv_ref[block * group : (block + 1) * group, tokens:, :].reshape(rows, 2 * HEAD)
        item = item.astype(f32)
        query, cot = item[:, :HEAD], item[:, HEAD:]
        query_scale = unit_scale(query)
        query_unit = (query * (query_scale * (gain * log2e))).astype(bf16)
        weight = jnp.exp2(dot_nt(key_s[...], query_unit)).astype(bf16)
        total = dot_nn(wide_t_s[...], weight).T
        inverse = 1.0 / total[:, HEAD:]
        out = total[:, :HEAD] * inverse
        grad = grad_ext(cot * inverse, out)
        slope = (weight.astype(f32) * dot_nt(wide_s[...], grad)).astype(bf16)
        gv = dot_nn(weight, grad)
        gk = dot_nn(slope, query_unit)
        if block == 0:
            gv_s[...] = gv
            gk_s[...] = gk
        else:
            gv_s[...] += gv
            gk_s[...] += gk
        gq = dot_nn(key_t_s[...], slope).T[:, :HEAD] * gain
        gq = unit_pull(query, query_scale, gq)
        result = jnp.concatenate([out, gq], axis=1).astype(bf16)
        back_ref[block * group : (block + 1) * group, tokens:, :] = result.reshape(
            group, share, 2 * HEAD
        )
    gk = unit_pull(key, key_scale, gk_s[...] * (1.0 / log2e))
    result = jnp.concatenate([gk, gv_s[:, :HEAD]], axis=1).astype(bf16)
    back_ref[:, 0:tokens, :] = result.reshape(sources, tokens, 2 * HEAD)


def low_backward(pos_ref, ret_ref, low_ref, cond_ref, cot_ref, *refs):
    weights = refs[:-8]
    output_ref, parts_ref, gmid_ref, proj_s, grad_s, merge_buf, low_buf, sems = refs[-8:]
    merge, lower = weight_copies(pos_ref, weights, merge_buf, low_buf, sems)
    for copy in lower[0] + lower[1] + merge[0] + merge[1]:
        copy.start()
    half_width = merge_buf.shape[4]
    core = pos_ref[1]
    places = [core * half_width, (1 - core) * half_width]
    tokens, width = low_ref.shape
    share = tokens // 2
    low = low_ref[...].astype(f32)
    for pair in range(width // (2 * HEAD)):
        outs, gqs, gks, gvs = [], [], [], []
        for head in (2 * pair, 2 * pair + 1):
            first, second = ret_ref[2 * head], ret_ref[2 * head + 1]
            sums = first[:tokens].astype(f32) + second[:tokens].astype(f32)
            gks.append(sums[:, :HEAD])
            gvs.append(sums[:, HEAD:])
            query = jnp.concatenate([first[tokens:], second[tokens:]], axis=0)
            outs.append(query[:, :HEAD])
            gqs.append(query[:, HEAD:])
        at = pair * 2 * HEAD
        out = jnp.concatenate(outs, axis=1).astype(f32)
        output_ref[:, at : at + 2 * HEAD] = (low[:, at : at + 2 * HEAD] + out).astype(bf16)
        proj_s[:, at : at + 2 * HEAD] = jnp.concatenate(gqs, axis=1)
        proj_s[:, width + at : width + at + 2 * HEAD] = jnp.concatenate(gks, axis=1).astype(bf16)
        proj_s[:, 2 * width + at : 2 * width + at + 2 * HEAD] = jnp.concatenate(
            gvs, axis=1
        ).astype(bf16)
    groups = parts_ref.shape[0]
    low_cols = 3 * width // groups
    for part in range(groups):
        parts_ref[part, :, 0:low_cols] = proj_s[:, part * low_cols : (part + 1) * low_cols]
    back = jnp.zeros((tokens, width), f32)
    for side in range(2):
        for copy in lower[side]:
            copy.wait()
        for block in range(3):
            place = pl.multiple_of(block * width + places[side], 128)
            back = back + dot_nt(
                proj_s[:, pl.ds(place, half_width)], low_block(low_buf, side, block)
            )
    grad = unit_pull(low, unit_scale(low), back * cond_ref[...])
    grad_s[...] = (cot_ref[...].astype(f32) + grad).astype(bf16)
    merge_cols = width // groups
    for part in range(groups):
        parts_ref[part, :, low_cols:] = grad_s[:, part * merge_cols : (part + 1) * merge_cols]
    wide = jnp.zeros((tokens, 4 * gmid_ref.shape[1]), f32)
    for side in range(2):
        for copy in merge[side]:
            copy.wait()
        place = pl.multiple_of(places[side], 128)
        wide = wide + dot_nt(grad_s[:, pl.ds(place, half_width)], merge_block(merge_buf, side))
    top = gmid_ref.shape[1]
    half = 16
    for row in range(2 * tokens // half):
        for odd in range(2):
            at = (2 * row + odd) * half
            low_at = (row // 2) * half
            place = (2 * (row % 2) + odd) * top
            gmid_ref[at : at + half, :] = wide[low_at : low_at + half, place : place + top]


def gather_top_grads(pos_ref, gq_ref, gmid_ref, prev_ref, next_ref, whole_ref, *refs):
    mine, theirs_ref, parts_s = refs[:-2], refs[-2], refs[-1]
    tokens, top = gq_ref.shape
    edge = prev_ref.shape[0]
    whole_ref[:, :top] = gq_ref[...]
    whole_ref[0:edge, top:] = (gmid_ref[0:edge] + prev_ref[...].astype(f32)).astype(bf16)
    whole_ref[edge : tokens - edge, top:] = gmid_ref[edge : tokens - edge].astype(bf16)
    whole_ref[tokens - edge :, top:] = (
        gmid_ref[tokens - edge :] + next_ref[...].astype(f32)
    ).astype(bf16)
    steps = len(mine)
    cols = whole_ref.shape[1] // (2 * steps)
    half = tokens // 2
    for part in range(2 * steps):
        step = lax.rem(part // 2 - pos_ref[4] + steps, steps)
        side = lax.rem(part + pos_ref[1], 2)
        at = part * cols
        parts_s[side, step, 0:tokens, :] = whole_ref[:, at : at + 128]
        rest = whole_ref[:, at + 128 : at + cols]
        parts_s[side, step, tokens:, :] = jnp.concatenate([rest[:half], rest[half:]], axis=1)
    for step in range(steps):
        mine[step][...] = parts_s[0, step]
    theirs_ref[...] = parts_s[1]


def product_low(normed_ref, unsh_ref, parts_ref, out_ref):
    devices = out_ref.shape[0]
    low_rows = normed_ref.shape[1] // devices
    merge_rows = unsh_ref.shape[1] // devices
    cols = parts_ref.shape[1] - 128
    part = dot_tn(unsh_ref[...], parts_ref[:, cols:]).astype(bf16)
    out_ref[:, 0:merge_rows, :] = part.reshape(devices, merge_rows, 128)
    part = dot_tn(normed_ref[...], parts_ref[:, :cols]).astype(bf16)
    for piece in range(cols // 128):
        at = merge_rows + piece * low_rows
        out_ref[:, at : at + low_rows, :] = part[:, piece * 128 : (piece + 1) * 128].reshape(
            devices, low_rows, 128
        )


def product_top(pos_ref, flat_ref, *refs):
    blocks, out_ref, first_s, rest_s = refs[:-3], refs[-3], refs[-2], refs[-1]
    steps = len(blocks) // 2
    tokens = flat_ref.shape[0] // len(blocks)
    half = tokens // 2
    for step in range(steps):
        y = lax.rem(pos_ref[4] + steps - step, steps)
        for side in range(2):
            core = lax.rem(pos_ref[1] + side, 2)
            at = pl.multiple_of((2 * y + core) * tokens, tokens)
            block = blocks[2 * step + side]
            first_s[pl.ds(at, tokens), :] = block[0:tokens, :]
            rest = block[tokens:, :]
            rest_s[pl.ds(at, tokens), :] = jnp.concatenate([rest[:, :64], rest[:, 64:]], axis=0)
    devices = out_ref.shape[0]
    rows = flat_ref.shape[1] // devices
    both = jnp.concatenate([first_s[...], rest_s[...]], axis=1)
    part = dot_tn(flat_ref[...], both).astype(bf16)
    out_ref[...] = part.reshape(devices, rows, part.shape[1])


def finish_tokens(pos_ref, whole_ref, tok_ref, cond_ref, grad_ref, own_ref, other_ref, out_ref):
    core = pos_ref[1]
    width = own_ref.shape[1]
    here = pl.multiple_of(core * width, 128)
    there = pl.multiple_of((1 - core) * width, 128)
    back = dot_nt(whole_ref[:, pl.ds(here, width)], own_ref[...])
    back = back + dot_nt(whole_ref[:, pl.ds(there, width)], other_ref[...])
    tok = tok_ref[...].astype(f32)
    out_ref[...] = (
        grad_ref[...] + unit_pull(tok, unit_scale(tok), back * cond_ref[...])
    ).astype(bf16)


def to_all(block, axis):
    return lax.all_to_all(block, axis, split_axis=0, concat_axis=0, tiled=True)


def spread(block, axis):
    count = lax.axis_size(axis)
    return lax.all_to_all(
        jnp.broadcast_to(block[None], (count,) + block.shape), axis, split_axis=0, concat_axis=0
    )


def around(block, axis):
    count = lax.axis_size(axis)
    return [block] + [
        lax.ppermute(block, axis, [(i, (i + step) % count) for i in range(count)])
        for step in range(1, count)
    ]


def swap_cores(block):
    return lax.ppermute(block, "c", [(0, 1), (1, 0)])


def body(
    image_tokens,
    top_cond,
    bottom_cond,
    top_qkv,
    top_scale,
    merge_weight,
    bottom_qkv,
    bottom_scale,
    out_cotangent,
):
    _, shard_rows, cols, top = image_tokens.shape
    width = bottom_cond.shape[1]
    row_devices = lax.axis_size(ROWS)
    images = lax.axis_size(DP)
    grid_rows = shard_rows * row_devices
    tokens = shard_rows * cols
    low_tokens = tokens // 4
    edge = 3 * cols
    row_at = lax.axis_index(ROWS)
    core = lax.axis_index("c")
    places = [row_at * shard_rows, core, row_at // 2, lax.axis_index("x"), lax.axis_index("y")]
    pos = jnp.stack(places).astype(jnp.int32)

    low_rows = bottom_qkv.shape[0]
    merge_rows = merge_weight.shape[0]
    half = width // 2
    merge_piece = lax.dynamic_slice_in_dim(merge_weight, core * half, half, 1)
    low_piece = jnp.concatenate(
        [bottom_qkv[:, i * width : (i + 1) * width] for i in range(3)], axis=0
    )
    low_piece = lax.dynamic_slice_in_dim(low_piece, core * half, half, 1)
    top_half = top_qkv.shape[1] // 2
    top_piece = lax.dynamic_slice_in_dim(top_qkv, core * top_half, top_half, 1)
    packed = jnp.stack(around(jnp.concatenate([merge_piece, low_piece], axis=0), "x"))
    tok = image_tokens[0].reshape(shard_rows, cols // 2, 2, top).transpose(0, 2, 1, 3)
    tok = tok.reshape(tokens, top)
    tok_f = tok.astype(f32)
    top_flat = (tok_f * unit_scale(tok_f) * top_cond[0]).astype(bf16)
    forward = [(i, i + 1) for i in range(row_devices - 1)]
    backward = [(i + 1, i) for i in range(row_devices - 1)]
    lo = lax.ppermute(top_flat[tokens - edge :], ROWS, forward)
    hi = lax.ppermute(top_flat[:edge], ROWS, backward)
    packed, lo, hi = lax.optimization_barrier((packed, lo, hi))
    w_own = lax.all_gather(packed, "z", axis=0, tiled=False)
    top_piece, _ = lax.optimization_barrier((top_piece, packed))
    top_own = spread(spread(top_piece, "z"), "x").reshape(top, top_half)
    top_other = swap_cores(top_own)

    ext = tokens + 2 * edge
    unshuffled, top_out, top_inv, proj = call(
        functools.partial(top_forward, grid_rows, cols),
        [smem(), smem()] + [vmem()] * 6,
        [
            ((low_tokens, 4 * top), bf16),
            ((tokens, top), f32),
            ((tokens, top), f32),
            ((ext, 3 * top), bf16),
        ],
        [pltpu.VMEM((tokens, ext), f32)],
        micros=6,
        name="top_forward",
    )(pos, top_scale, tok, top_flat, lo, hi, top_own, top_other)

    unshuffled, top_flat_late, w_own = lax.optimization_barrier((unshuffled, top_flat, w_own))
    weights = (w_own, swap_cores(w_own))

    cot = out_cotangent[0].reshape(low_tokens, width)
    ring = (lax.axis_size("x"), lax.axis_size("z"))
    weight_scratch = [
        pltpu.VMEM((2,) + ring + (merge_rows, half), bf16),
        pltpu.VMEM((2,) + ring + (3 * low_rows, half), bf16),
        pltpu.SemaphoreType.DMA((2, 2 * ring[0])),
    ]
    exchange = (row_devices, low_tokens * 3 // 2, 2 * HEAD)
    low, low_normed, send = call(
        low_forward,
        [smem()] + [vmem()] * 3 + [anywhere()] * len(weights),
        [((low_tokens, width), bf16), ((low_tokens, width), bf16), (exchange, bf16)],
        [pltpu.VMEM((low_tokens, 3 * width), bf16)] + weight_scratch,
        limit=60,
        micros=5,
        name="low_forward",
    )(pos, unshuffled, bottom_cond, cot, *weights)
    recv = to_all(send, ROWS)
    keys = row_devices * low_tokens
    (back,) = call(
        low_attend,
        [smem(), smem(), vmem()],
        [(exchange, bf16)],
        [
            pltpu.VMEM((keys, HEAD), bf16),
            pltpu.VMEM((2 * HEAD, keys), bf16),
            pltpu.VMEM((keys, 2 * HEAD), bf16),
            pltpu.VMEM((2 * HEAD, keys), bf16),
            pltpu.VMEM((keys, HEAD), f32),
            pltpu.VMEM((keys, 2 * HEAD), f32),
        ],
        micros=11,
        name="low_attend",
    )(pos, bottom_scale, recv)
    ret = to_all(back, ROWS)
    low_cols, merge_cols = 3 * width // images, width // images
    output, low_parts, grad_middle = call(
        low_backward,
        [smem()] + [vmem()] * 4 + [anywhere()] * len(weights),
        [
            ((low_tokens, width), bf16),
            ((images, low_tokens, low_cols + merge_cols), bf16),
            ((tokens, top), f32),
        ],
        [pltpu.VMEM((low_tokens, 3 * width), bf16), pltpu.VMEM((low_tokens, width), bf16)]
        + weight_scratch,
        limit=60,
        micros=6,
        name="low_backward",
    )(pos, ret, low, bottom_cond, cot, *weights)
    low_parts = to_all(low_parts, DP).reshape(images * low_tokens, low_cols + merge_cols)

    gq, gmid, gup, gdown = call(
        functools.partial(top_backward, grid_rows, cols),
        [smem(), smem()] + [vmem()] * 4,
        [
            ((tokens, top), bf16),
            ((tokens, 2 * top), f32),
            ((edge, 2 * top), bf16),
            ((edge, 2 * top), bf16),
        ],
        [pltpu.VMEM((tokens + 2 * edge, tokens), f32)],
        micros=13,
        name="top_backward",
    )(pos, top_scale, proj, top_out, top_inv, grad_middle)
    gup, gdown, low_parts = lax.optimization_barrier((gup, gdown, low_parts))
    from_next = lax.ppermute(gup, ROWS, backward)
    from_prev = lax.ppermute(gdown, ROWS, forward)

    top_all = lax.all_gather(top_flat_late, DP, axis=0, tiled=True)
    unsh_all = lax.all_gather(unshuffled, DP, axis=0, tiled=True)
    normed_all = lax.all_gather(low_normed, DP, axis=0, tiled=True)
    (sums,) = call(
        product_low,
        [vmem()] * 3,
        [((row_devices, merge_rows + 3 * width // images * low_rows // 128, 128), bf16)],
        micros=4,
        name="product_low",
    )(normed_all, unsh_all, low_parts)
    sums, gq, from_prev, from_next = lax.optimization_barrier((sums, gq, from_prev, from_next))
    steps = images // 2
    grad_top, *mine, theirs = call(
        gather_top_grads,
        [smem()] + [vmem()] * 4,
        [((tokens, 3 * top), bf16)]
        + [((tokens * 3 // 2, 128), bf16)] * steps
        + [((steps, tokens * 3 // 2, 128), bf16)],
        [pltpu.VMEM((2, steps, tokens * 3 // 2, 128), bf16)],
        name="gather_top_grads",
    )(pos, gq, gmid, from_prev, from_next)
    (grad_tokens,) = call(
        finish_tokens,
        [smem()] + [vmem()] * 6,
        [((tokens, top), bf16)],
        name="finish_tokens",
    )(pos, grad_top, tok, top_cond, grad_middle, top_own, top_other)
    sums = to_all(sums, ROWS)

    def along_y(block, step):
        if step == 0:
            return block
        return lax.ppermute(block, "y", [(i, (i + step) % steps) for i in range(steps)])

    mine = [along_y(block, step) for step, block in enumerate(mine)]
    theirs = swap_cores(theirs)
    theirs = [along_y(theirs[step], step) for step in range(steps)]
    top_cols = 3 * top // images
    (part_top,) = call(
        product_top,
        [smem()] + [vmem()] * (1 + images),
        [((row_devices, top // row_devices, top_cols), bf16)],
        [pltpu.VMEM((images * tokens, 128), bf16), pltpu.VMEM((images * tokens, 64), bf16)],
        micros=3,
        name="product_top",
    )(pos, top_all, *[block for pair in zip(mine, theirs) for block in pair])
    part_top, sums = lax.optimization_barrier((part_top, sums))
    part_top = to_all(part_top, ROWS)
    sum_top = jnp.sum(part_top.astype(f32), axis=0)
    sums = jnp.sum(sums.astype(f32), axis=0)
    sum_merge = sums[:merge_rows]
    pieces = low_cols // 128
    sum_low = sums[merge_rows:].reshape(pieces, low_rows, 128).transpose(1, 0, 2)
    sum_low = sum_low.reshape(low_rows, pieces * 128)

    grad_tokens = grad_tokens.reshape(shard_rows, 2, cols // 2, top).transpose(0, 2, 1, 3)
    return (
        output.reshape(1, shard_rows // 2, cols // 2, width),
        grad_tokens.reshape(1, shard_rows, cols, top),
        sum_top,
        sum_merge,
        sum_low,
    )


def solution(mesh):
    images, row_devices = mesh.shape["dp"], mesh.shape["rows"]
    grid = mesh.devices.reshape(images // 2, 2, row_devices // 8, 8)
    split = Mesh(grid, ("y", "c", "x", "z"))
    placed = (
        P(DP, ROWS, None, None),
        P(DP, None),
        P(DP, None),
        P(ROWS, None),
        P(),
        P(ROWS, None),
        P(ROWS, None),
        P(),
        P(DP, ROWS, None, None),
    )
    return jax.shard_map(
        body,
        mesh=split,
        in_specs=placed,
        out_specs=(
            P(DP, ROWS, None, None),
            P(DP, ROWS, None, None),
            P(ROWS, DP),
            P(ROWS, DP),
            P(ROWS, DP),
        ),
        check_vma=False,
    )
```

```python
import functools
import jax
import jax.numpy as jnp
from jax import lax
from jax.experimental import pallas as pl
from jax.experimental.pallas import tpu as pltpu
from jax.sharding import Mesh, PartitionSpec as P

epsilon = 1e-06
log2e = 1.4426950408889634
f32 = jnp.float32
bf16 = jnp.bfloat16
ROWS = ("x", "z")
DP = ("y", "c")
HEAD = 64
MIB = 1 << 20
DP_STEPS = 4


def dot_nn(left, right):
    return jnp.dot(left, right, preferred_element_type=f32)


def dot_nt(left, right):
    return lax.dot_general(left, right, (((1,), (1,)), ((), ())), preferred_element_type=f32)


def dot_tn(left, right):
    return lax.dot_general(left, right, (((0,), (0,)), ((), ())), preferred_element_type=f32)


def unit_scale(x):
    return lax.rsqrt(jnp.mean(x * x, axis=-1, keepdims=True) + epsilon)


def unit_pull(x, scale, grad):
    inner = jnp.mean(x * grad, axis=-1, keepdims=True)
    return scale * grad - x * (scale * scale * scale * inner)


def grad_ext(grad, out):
    delta = jnp.sum(grad * out, axis=-1, keepdims=True)
    high = delta.astype(bf16).astype(f32)
    rest = delta - high
    lane = lax.broadcasted_iota(jnp.int32, grad.shape, 1)
    tail = jnp.where(lane == 0, -high, jnp.where(lane == 1, -rest, 0.0))
    return jnp.concatenate([grad, tail], axis=1).astype(bf16)


def vmem():
    return pl.BlockSpec(memory_space=pltpu.VMEM)


def smem():
    return pl.BlockSpec(memory_space=pltpu.SMEM)


def fetch(sources, targets, sems):
    copies = [
        pltpu.make_async_copy(source, target, sems.at[index])
        for index, (source, target) in enumerate(zip(sources, targets))
    ]
    for copy in copies:
        copy.start()
    return copies


def row_pieces(ref, count):
    rows = ref.shape[0] // count
    return [ref.at[i * rows : (i + 1) * rows] for i in range(count)]


def anywhere():
    return pl.BlockSpec(memory_space=pl.ANY)


def call(kernel, ins, outs, scratch=(), limit=40, micros=2, name=None):
    return pl.pallas_call(
        kernel,
        in_specs=ins,
        out_specs=[vmem() for _ in outs],
        out_shape=[jax.ShapeDtypeStruct(shape, kind) for shape, kind in outs],
        scratch_shapes=list(scratch),
        compiler_params=pltpu.CompilerParams(vmem_limit_bytes=limit * MIB),
        cost_estimate=pl.CostEstimate(
            flops=micros * 1000000000, bytes_accessed=micros * 3000000, transcendentals=0
        ),
        name=name,
    )


def neighbour_mask(first, grid_rows, cols, query_dim, shape):
    query = lax.broadcasted_iota(jnp.int32, shape, query_dim)
    key = lax.broadcasted_iota(jnp.int32, shape, 1 - query_dim)
    half = cols // 2

    def column(index):
        place = index % cols
        return 2 * (place % half) + place // half

    shift = key // cols - query // cols
    apart = column(key) - column(query)
    key_row = first - 3 + key // cols
    inside = (shift >= 0) & (shift <= 6) & (apart >= -3) & (apart <= 3)
    inside = inside & (key_row >= 0) & (key_row < grid_rows)
    return jnp.where(inside, 1.0, 0.0).astype(f32)


def head_parts(proj_ref, at, top, tokens):
    edge = (proj_ref.shape[0] - tokens) // 2
    query = proj_ref[edge : edge + tokens, at : at + HEAD].astype(f32)
    key = proj_ref[:, top + at : top + at + HEAD].astype(f32)
    value = proj_ref[:, 2 * top + at : 2 * top + at + HEAD]
    return query, key, value


def top_forward(
    grid_rows, cols, pos_ref, scale_ref, tok_ref, flat_ref, lo_ref, hi_ref, own_ref, other_ref,
    unsh_ref, out_ref, inv_ref, proj_ref, ext_ref, mask_ref,
):
    tokens, top = tok_ref.shape
    core = pos_ref[1]
    width = own_ref.shape[1]
    ext = jnp.concatenate([lo_ref[...], flat_ref[...], hi_ref[...]], axis=0)
    ext_ref[...] = ext
    here = pl.multiple_of(core * width, 128)
    there = pl.multiple_of((1 - core) * width, 128)
    proj_ref[:, pl.ds(here, width)] = dot_nn(ext, own_ref[...]).astype(bf16)
    proj_ref[:, pl.ds(there, width)] = dot_nn(ext, other_ref[...]).astype(bf16)
    mask_ref[...] = neighbour_mask(pos_ref[0], grid_rows, cols, 0, mask_ref.shape)
    for pair in range(top // (2 * HEAD)):
        outs, invs = [], []
        for head in (2 * pair, 2 * pair + 1):
            query, key, value = head_parts(proj_ref, head * HEAD, top, tokens)
            gain = scale_ref[head] * (log2e / HEAD)
            query = (query * (unit_scale(query) * gain)).astype(bf16)
            key = (key * unit_scale(key)).astype(bf16)
            wide = jnp.concatenate([value, jnp.ones_like(value)], axis=1)
            weight = (jnp.exp2(dot_nt(query, key)) * mask_ref[...]).astype(bf16)
            both = dot_nn(weight, wide)
            inverse = 1.0 / both[:, HEAD:]
            outs.append(both[:, :HEAD] * inverse)
            invs.append(inverse)
        at = pair * 2 * HEAD
        out_ref[:, at : at + 2 * HEAD] = jnp.concatenate(outs, axis=1)
        inv_ref[:, at : at + 2 * HEAD] = jnp.concatenate(invs, axis=1)
    half = cols // 2
    for row in range(tok_ref.shape[0] // cols):
        for odd in range(2):
            at = row * cols + odd * half
            part = tok_ref[at : at + half, :].astype(f32) + out_ref[at : at + half, :]
            low_at = (row // 2) * half
            place = (2 * (row % 2) + odd) * top
            unsh_ref[low_at : low_at + half, place : place + top] = part.astype(bf16)


def top_backward(
    grid_rows, cols, first_pair, pos_ref, scale_ref, grad_ref, proj_any, out_any, inv_any,
    whole_ref, mask_ref, proj_ref, out_ref, inv_ref, sems,
):
    tokens, width = out_ref.shape
    ext, top = whole_ref.shape[0], proj_any.shape[1] // 3
    start = first_pair * 2 * HEAD
    sources = [proj_any.at[:, i * top + start : i * top + start + width] for i in range(3)]
    sources += [ref.at[:, start : start + width] for ref in (out_any, inv_any)]
    targets = [proj_ref.at[:, i * width : (i + 1) * width] for i in range(3)]
    copies = fetch(sources, targets + [out_ref, inv_ref], sems)
    edge = (ext - tokens) // 2
    blank = jnp.zeros((edge, width), bf16)
    whole_ref[:edge, :width] = blank
    whole_ref[edge + tokens :, :width] = blank
    mask_ref[...] = neighbour_mask(pos_ref[0], grid_rows, cols, 1, mask_ref.shape)
    for copy in copies:
        copy.wait()
    for pair in range(width // (2 * HEAD)):
        gqs, gks, gvs = [], [], []
        for head in (2 * pair, 2 * pair + 1):
            at = head * HEAD
            query, key, value = head_parts(proj_ref, at, width, tokens)
            gain = scale_ref[2 * first_pair + head] * (1.0 / HEAD)
            query_scale = unit_scale(query)
            key_scale = unit_scale(key)
            query_unit = (query * (query_scale * (gain * log2e))).astype(bf16)
            key_f = key * key_scale
            key_unit = key_f.astype(bf16)
            key_t = jnp.concatenate([key_f, jnp.zeros_like(key_f)], axis=1).T.astype(bf16)
            wide = jnp.concatenate([value, jnp.ones_like(value)], axis=1)
            grad = grad_ref[:, start + at : start + at + HEAD] * inv_ref[:, at : at + HEAD]
            grad = grad_ext(grad, out_ref[:, at : at + HEAD])
            weight = jnp.exp2(dot_nt(key_unit, query_unit)) * mask_ref[...]
            slope = (weight * dot_nt(wide, grad)).astype(bf16)
            gvs.append(dot_nn(weight.astype(bf16), grad)[:, :HEAD])
            gk = dot_nn(slope, query_unit) * (1.0 / log2e)
            gks.append(unit_pull(key, key_scale, gk))
            gq = dot_nn(key_t, slope).T[:, :HEAD] * gain
            gqs.append(unit_pull(query, query_scale, gq))
        at = pair * 2 * HEAD
        gq = jnp.concatenate(gqs, axis=1).astype(bf16)
        whole_ref[edge : edge + tokens, at : at + 2 * HEAD] = gq
        for base, parts in ((width + at, gks), (2 * width + at, gvs)):
            whole = jnp.concatenate(parts, axis=1).astype(bf16)
            whole_ref[:, base : base + 2 * HEAD] = whole


def top_backward_rest(
    grid_rows, cols, first_pair, pos_ref, scale_ref, grad_ref, prior_ref,
    proj_any, out_any, inv_any, whole_ref, up_ref, down_ref, *refs,
):
    mine, refs = refs[:DP_STEPS], refs[DP_STEPS:]
    theirs_ref, parts_s, here_s = refs[:3]
    top_backward(
        grid_rows, cols, first_pair, pos_ref, scale_ref, grad_ref, proj_any, out_any, inv_any,
        here_s, *refs[3:],
    )
    rows, width = here_s.shape[0], here_s.shape[1] // 3
    edge = up_ref.shape[0]
    top = 2 * width
    for block in range(3):
        for side, ref in enumerate((prior_ref, here_s)):
            at = (2 * block + side) * width
            whole_ref[:, at : at + width] = ref[:, block * width : (block + 1) * width]
    up_ref[...] = whole_ref[:edge, top:]
    down_ref[...] = whole_ref[rows - edge :, top:]
    part_cols = whole_ref.shape[1] // (2 * DP_STEPS)
    half = rows // 2
    for part in range(2 * DP_STEPS):
        step = lax.rem(part // 2 - pos_ref[4] + DP_STEPS, DP_STEPS)
        side = lax.rem(part + pos_ref[1], 2)
        at = part * part_cols
        parts_s[side, step, 0:rows, :] = whole_ref[:, at : at + 128]
        rest = whole_ref[:, at + 128 : at + part_cols]
        parts_s[side, step, rows:, :] = jnp.concatenate([rest[:half], rest[half:]], axis=1)
    for step in range(DP_STEPS):
        mine[step][...] = parts_s[0, step]
    theirs_ref[...] = parts_s[1]


def weight_copies(pos_ref, weights, merge_buf, low_buf, sems):
    steps_x, rows_low = low_buf.shape[1], low_buf.shape[3]
    steps_y = DP_STEPS
    rows = merge_buf.shape[3] // steps_y
    half_rows, cols = merge_buf.shape[3] // 2, merge_buf.shape[4] // 2
    merge, low = [[], []], [[], []]
    for side in range(2):
        for step in range(steps_y):
            place = lax.rem(pos_ref[4] + steps_y - step, steps_y) * rows
            merge[side].append(
                pltpu.make_async_copy(
                    weights[side * steps_y + step],
                    merge_buf.at[side, :, :, pl.ds(pl.multiple_of(place, rows), rows), 0:cols],
                    sems.at[side, step],
                )
            )
        rest = weights[2 * steps_y + side]
        for step in range(steps_x):
            place = lax.rem(pos_ref[3] + steps_x - step, steps_x)
            for part in range(2):
                merge[side].append(
                    pltpu.make_async_copy(
                        rest.at[:, step, rows_low:, part * cols : (part + 1) * cols],
                        merge_buf.at[
                            side, place, :, part * half_rows : (part + 1) * half_rows, cols:
                        ],
                        sems.at[side, steps_y + 3 * step + part],
                    )
                )
            low[side].append(
                pltpu.make_async_copy(
                    rest.at[:, step, 0:rows_low, :],
                    low_buf.at[side, place],
                    sems.at[side, steps_y + 3 * step + 2],
                )
            )
    return merge, low


def merge_block(merge_buf, side):
    part = merge_buf[side]
    return part.reshape(part.shape[0] * part.shape[1] * part.shape[2], part.shape[3])


def low_block(low_buf, side, block):
    rows = low_buf.shape[3] // 3
    part = low_buf[side, :, :, block * rows : (block + 1) * rows, :]
    return part.reshape(part.shape[0] * part.shape[1] * rows, part.shape[3])


def low_forward(pos_ref, unsh_ref, cond_ref, cot_ref, *refs):
    weights, (low_ref, normed_ref, send_ref, proj_s, merge_buf, low_buf, sems) = refs[:-7], refs[-7:]
    merge, lower = weight_copies(pos_ref, weights, merge_buf, low_buf, sems)
    for copy in merge[0] + merge[1] + lower[0] + lower[1]:
        copy.start()
    half = merge_buf.shape[4]
    width = 2 * half
    core = pos_ref[1]
    places = [core * half, (1 - core) * half]
    for side in range(2):
        for copy in merge[side]:
            copy.wait()
        place = pl.multiple_of(places[side], 128)
        low_ref[:, pl.ds(place, half)] = dot_nn(
            unsh_ref[...], merge_block(merge_buf, side)
        ).astype(bf16)
    low = low_ref[...].astype(f32)
    normed = (low * unit_scale(low) * cond_ref[...]).astype(bf16)
    normed_ref[...] = normed
    for side in range(2):
        for copy in lower[side]:
            copy.wait()
        for block in range(3):
            place = pl.multiple_of(block * width + places[side], 128)
            proj_s[:, pl.ds(place, half)] = dot_nn(
                normed, low_block(low_buf, side, block)
            ).astype(bf16)
    query, key, value = (proj_s[:, i * width : (i + 1) * width] for i in range(3))
    tokens = query.shape[0]
    share = tokens // 4
    for head in range(query.shape[1] // HEAD):
        at = head * HEAD
        key_value = jnp.concatenate([key[:, at : at + HEAD], value[:, at : at + HEAD]], axis=1)
        for part in range(2):
            send_ref[2 * head + part, 0:tokens, :] = key_value
            for index, rows in enumerate((query, cot_ref)):
                first = 2 * part * share
                send_ref[2 * head + part, tokens + index * share : tokens + (index + 1) * share] = (
                    jnp.concatenate(
                        [
                            rows[first : first + share, at : at + HEAD],
                            rows[first + share : first + 2 * share, at : at + HEAD],
                        ],
                        axis=1,
                    )
                )


def two_shares(ref_value):
    sources, share, lanes = ref_value.shape
    both = ref_value.reshape(sources * share, lanes).astype(f32)
    return jnp.concatenate([both[:, :HEAD], both[:, HEAD:]], axis=0)


def low_attend(
    pos_ref, scale_ref, recv_ref, back_ref, key_s, key_t_s, wide_s, wide_t_s, gk_s, gv_s,
):
    gain = scale_ref[pos_ref[2]] * (1.0 / HEAD)
    sources = recv_ref.shape[0]
    share = recv_ref.shape[1] // 6
    tokens = 4 * share
    keys = sources * tokens
    both = recv_ref[:, 0:tokens, :].reshape(keys, 2 * HEAD)
    key = both[:, :HEAD].astype(f32)
    key_scale = unit_scale(key)
    key_f = key * key_scale
    key_s[...] = key_f.astype(bf16)
    key_t_s[...] = jnp.concatenate([key_f, jnp.zeros_like(key_f)], axis=1).T.astype(bf16)
    wide = jnp.concatenate([both[:, HEAD:].astype(f32), jnp.ones_like(key_f)], axis=1)
    wide_s[...] = wide.astype(bf16)
    wide_t_s[...] = wide.T.astype(bf16)
    group = 8
    rows = group * share
    for block in range(sources // group):
        at = block * group
        query = two_shares(recv_ref[at : at + group, tokens : tokens + share, :])
        cot = two_shares(recv_ref[at : at + group, tokens + share :, :])
        query_scale = unit_scale(query)
        query_unit = (query * (query_scale * (gain * log2e))).astype(bf16)
        weight = jnp.exp2(dot_nt(key_s[...], query_unit)).astype(bf16)
        total = dot_nn(wide_t_s[...], weight).T
        inverse = 1.0 / total[:, HEAD:]
        out = total[:, :HEAD] * inverse
        grad = grad_ext(cot * inverse, out)
        slope = (weight.astype(f32) * dot_nt(wide_s[...], grad)).astype(bf16)
        gv = dot_nn(weight, grad)
        gk = dot_nn(slope, query_unit)
        if block == 0:
            gv_s[...] = gv
            gk_s[...] = gk
        else:
            gv_s[...] += gv
            gk_s[...] += gk
        gq = dot_nn(key_t_s[...], slope).T[:, :HEAD] * gain
        gq = unit_pull(query, query_scale, gq)
        result = jnp.concatenate([out, gq], axis=1).astype(bf16)
        for part in range(2):
            back_ref[at : at + group, tokens + part * share : tokens + (part + 1) * share, :] = (
                result[part * rows : (part + 1) * rows].reshape(group, share, 2 * HEAD)
            )
    gk = unit_pull(key, key_scale, gk_s[...] * (1.0 / log2e))
    result = jnp.concatenate([gk, gv_s[:, :HEAD]], axis=1).astype(bf16)
    back_ref[:, 0:tokens, :] = result.reshape(sources, tokens, 2 * HEAD)


def low_backward(pos_ref, ret_ref, low_ref, cond_ref, cot_ref, *refs):
    weights = refs[:-8]
    output_ref, parts_ref, gmid_ref, proj_s, grad_s, merge_buf, low_buf, sems = refs[-8:]
    merge, lower = weight_copies(pos_ref, weights, merge_buf, low_buf, sems)
    for copy in lower[0] + lower[1] + merge[0] + merge[1]:
        copy.start()
    half_width = merge_buf.shape[4]
    core = pos_ref[1]
    places = [core * half_width, (1 - core) * half_width]
    tokens, width = low_ref.shape
    share = tokens // 2
    low = low_ref[...].astype(f32)
    for pair in range(width // (2 * HEAD)):
        outs, gqs, gks, gvs = [], [], [], []
        for head in (2 * pair, 2 * pair + 1):
            first, second = ret_ref[2 * head], ret_ref[2 * head + 1]
            sums = first[:tokens].astype(f32) + second[:tokens].astype(f32)
            gks.append(sums[:, :HEAD])
            gvs.append(sums[:, HEAD:])
            query = jnp.concatenate([first[tokens:], second[tokens:]], axis=0)
            outs.append(query[:, :HEAD])
            gqs.append(query[:, HEAD:])
        at = pair * 2 * HEAD
        out = jnp.concatenate(outs, axis=1).astype(f32)
        output_ref[:, at : at + 2 * HEAD] = (low[:, at : at + 2 * HEAD] + out).astype(bf16)
        proj_s[:, at : at + 2 * HEAD] = jnp.concatenate(gqs, axis=1)
        proj_s[:, width + at : width + at + 2 * HEAD] = jnp.concatenate(gks, axis=1).astype(bf16)
        proj_s[:, 2 * width + at : 2 * width + at + 2 * HEAD] = jnp.concatenate(
            gvs, axis=1
        ).astype(bf16)
    groups = parts_ref.shape[0]
    low_cols = 3 * width // groups
    for part in range(groups):
        parts_ref[part, :, 0:low_cols] = proj_s[:, part * low_cols : (part + 1) * low_cols]
    back = jnp.zeros((tokens, width), f32)
    for side in range(2):
        for copy in lower[side]:
            copy.wait()
        for block in range(3):
            place = pl.multiple_of(block * width + places[side], 128)
            back = back + dot_nt(
                proj_s[:, pl.ds(place, half_width)], low_block(low_buf, side, block)
            )
    grad = unit_pull(low, unit_scale(low), back * cond_ref[...])
    grad_s[...] = (cot_ref[...].astype(f32) + grad).astype(bf16)
    merge_cols = width // groups
    for part in range(groups):
        parts_ref[part, :, low_cols:] = grad_s[:, part * merge_cols : (part + 1) * merge_cols]
    wide = jnp.zeros((tokens, 4 * gmid_ref.shape[1]), f32)
    for side in range(2):
        for copy in merge[side]:
            copy.wait()
        place = pl.multiple_of(places[side], 128)
        wide = wide + dot_nt(grad_s[:, pl.ds(place, half_width)], merge_block(merge_buf, side))
    top = gmid_ref.shape[1]
    half = 16
    for row in range(2 * tokens // half):
        for odd in range(2):
            at = (2 * row + odd) * half
            low_at = (row // 2) * half
            place = (2 * (row % 2) + odd) * top
            gmid_ref[at : at + half, :] = wide[low_at : low_at + half, place : place + top]


def product_low(parts_ref, unsh_any, normed_any, out_ref, unsh_ref, normed_ref, sems):
    pieces = 4
    sources = row_pieces(unsh_any, pieces) + row_pieces(normed_any, pieces)
    copies = fetch(sources, row_pieces(unsh_ref, pieces) + row_pieces(normed_ref, pieces), sems)
    devices = out_ref.shape[0]
    low_rows = normed_ref.shape[1] // devices
    merge_rows = unsh_ref.shape[1] // devices
    cols = parts_ref.shape[1] - 128
    for copy in copies[:pieces]:
        copy.wait()
    part = dot_tn(unsh_ref[...], parts_ref[:, cols:]).astype(bf16)
    out_ref[:, 0:merge_rows, :] = part.reshape(devices, merge_rows, 128)
    for copy in copies[pieces:]:
        copy.wait()
    part = dot_tn(normed_ref[...], parts_ref[:, :cols]).astype(bf16)
    for piece in range(cols // 128):
        at = merge_rows + piece * low_rows
        out_ref[:, at : at + low_rows, :] = part[:, piece * 128 : (piece + 1) * 128].reshape(
            devices, low_rows, 128
        )


def product_top(pos_ref, flat_any, *refs):
    blocks, out_ref, first_s, rest_s, flat_ref, blocks_s, sems = refs[:-6], *refs[-6:]
    steps = len(blocks) // 2
    count = len(blocks)
    copies = fetch(
        list(blocks) + row_pieces(flat_any, count),
        [blocks_s.at[index] for index in range(count)] + row_pieces(flat_ref, count),
        sems,
    )
    tokens = flat_ref.shape[0] // len(blocks)
    for step in range(steps):
        y = lax.rem(pos_ref[4] + steps - step, steps)
        for side in range(2):
            core = lax.rem(pos_ref[1] + side, 2)
            at = pl.multiple_of((2 * y + core) * tokens, 16)
            copies[2 * step + side].wait()
            block = blocks_s[2 * step + side]
            first_s[pl.ds(at, tokens), :] = block[0:tokens, :]
            rest = block[tokens:, :]
            rest_s[pl.ds(at, tokens), :] = jnp.concatenate([rest[:, :64], rest[:, 64:]], axis=0)
    devices = out_ref.shape[0]
    rows = flat_ref.shape[1] // devices
    both = jnp.concatenate([first_s[...], rest_s[...]], axis=1)
    for copy in copies[count:]:
        copy.wait()
    part = dot_tn(flat_ref[...], both).astype(bf16)
    out_ref[...] = part.reshape(devices, rows, part.shape[1])


def finish_tokens(
    pos_ref, whole_ref, prev_ref, next_ref, tok_ref, cond_ref, grad_ref, own_ref, other_ref,
    out_ref, sum_s,
):
    tokens, top = tok_ref.shape
    edge = prev_ref.shape[0]
    sum_s[...] = whole_ref[edge : edge + tokens, :]
    for at, ref in ((0, prev_ref), (tokens - edge, next_ref)):
        part = sum_s[at : at + edge, top:].astype(f32) + ref[...].astype(f32)
        sum_s[at : at + edge, top:] = part.astype(bf16)
    core = pos_ref[1]
    width = own_ref.shape[1]
    here = pl.multiple_of(core * width, 128)
    there = pl.multiple_of((1 - core) * width, 128)
    back = dot_nt(sum_s[:, pl.ds(here, width)], own_ref[...])
    back = back + dot_nt(sum_s[:, pl.ds(there, width)], other_ref[...])
    tok = tok_ref[...].astype(f32)
    out_ref[...] = (
        grad_ref[...] + unit_pull(tok, unit_scale(tok), back * cond_ref[...])
    ).astype(bf16)


def to_all(block, axis):
    return lax.all_to_all(block, axis, split_axis=0, concat_axis=0, tiled=True)


def spread(block, axis):
    count = lax.axis_size(axis)
    return lax.all_to_all(
        jnp.broadcast_to(block[None], (count,) + block.shape), axis, split_axis=0, concat_axis=0
    )


def around(block, axis):
    count = lax.axis_size(axis)
    return [block] + [
        lax.ppermute(block, axis, [(i, (i + step) % count) for i in range(count)])
        for step in range(1, count)
    ]


def swap_cores(block):
    return lax.ppermute(block, "c", [(0, 1), (1, 0)])


def body(
    image_tokens,
    top_cond,
    bottom_cond,
    top_qkv,
    top_scale,
    merge_weight,
    bottom_qkv,
    bottom_scale,
    out_cotangent,
):
    _, shard_rows, cols, top = image_tokens.shape
    width = bottom_cond.shape[1]
    row_devices = lax.axis_size(ROWS)
    images = lax.axis_size(DP)
    grid_rows = shard_rows * row_devices
    tokens = shard_rows * cols
    low_tokens = tokens // 4
    edge = 3 * cols
    row_at = lax.axis_index(ROWS)
    core = lax.axis_index("c")
    places = [row_at * shard_rows, core, row_at // 2, lax.axis_index("x"), lax.axis_index("y")]
    pos = jnp.stack(places).astype(jnp.int32)

    low_rows = bottom_qkv.shape[0]
    merge_rows = merge_weight.shape[0]
    half = width // 2
    merge_piece = lax.dynamic_slice_in_dim(merge_weight, core * half, half, 1)
    low_piece = jnp.concatenate(
        [bottom_qkv[:, i * width : (i + 1) * width] for i in range(3)], axis=0
    )
    low_piece = lax.dynamic_slice_in_dim(low_piece, core * half, half, 1)
    top_half = top_qkv.shape[1] // 2
    top_piece = lax.dynamic_slice_in_dim(top_qkv, core * top_half, top_half, 1)
    merge_side = merge_piece[:, half // 2 :]
    merge_side = jnp.concatenate(
        [merge_side[: merge_rows // 2], merge_side[merge_rows // 2 :]], axis=1
    )
    packed = jnp.stack(around(jnp.concatenate([low_piece, merge_side], axis=0), "x"))
    tok = image_tokens[0].reshape(shard_rows, cols // 2, 2, top).transpose(0, 2, 1, 3)
    tok = tok.reshape(tokens, top)
    tok_f = tok.astype(f32)
    top_flat = (tok_f * unit_scale(tok_f) * top_cond[0]).astype(bf16)
    forward = [(i, i + 1) for i in range(row_devices - 1)]
    backward = [(i + 1, i) for i in range(row_devices - 1)]
    lo = lax.ppermute(top_flat[tokens - edge :], ROWS, forward)
    hi = lax.ppermute(top_flat[:edge], ROWS, backward)
    packed = lax.optimization_barrier(packed)
    w_own = lax.all_gather(packed, "z", axis=0, tiled=False)
    steps = lax.axis_size("y")
    quarter = merge_rows // steps
    merge_piece = lax.dynamic_slice(
        merge_piece, (lax.axis_index("y") * quarter, 0), (quarter, half // 2)
    )
    first = jnp.concatenate([top_piece, merge_piece], axis=1)
    first, _ = lax.optimization_barrier((first, packed))
    first = spread(first, "z")
    first, lo, hi = lax.optimization_barrier((first, lo, hi))
    first = spread(first, "x")
    top_own = first[..., :top_half].reshape(top, top_half)
    top_other = swap_cores(top_own)
    merge_own = around(first[..., top_half:], "y")
    merge_other = [swap_cores(block) for block in merge_own]
    top_own, w_own, *merge_both = lax.optimization_barrier(
        (top_own, w_own, *merge_own, *merge_other)
    )

    ext = tokens + 2 * edge
    unshuffled, top_out, top_inv, proj, top_ext = call(
        functools.partial(top_forward, grid_rows, cols),
        [smem(), smem()] + [vmem()] * 6,
        [
            ((low_tokens, 4 * top), bf16),
            ((tokens, top), f32),
            ((tokens, top), f32),
            ((ext, 3 * top), bf16),
            ((ext, top), bf16),
        ],
        [pltpu.VMEM((tokens, ext), f32)],
        micros=6,
        name="top_forward",
    )(pos, top_scale, tok, top_flat, lo, hi, top_own, top_other)

    weights = (*merge_both, w_own, swap_cores(w_own))

    ring = (lax.axis_size("x"), lax.axis_size("z"))
    weight_scratch = [
        pltpu.VMEM((2,) + ring + (merge_rows, half), bf16),
        pltpu.VMEM((2,) + ring + (3 * low_rows, half), bf16),
        pltpu.SemaphoreType.DMA((2, steps + 3 * ring[0])),
    ]
    cot = out_cotangent[0].reshape(low_tokens, width)
    exchange = (row_devices, low_tokens * 3 // 2, 2 * HEAD)
    low, low_normed, send = call(
        low_forward,
        [smem()] + [vmem()] * 3 + [anywhere()] * len(weights),
        [((low_tokens, width), bf16), ((low_tokens, width), bf16), (exchange, bf16)],
        [pltpu.VMEM((low_tokens, 3 * width), bf16)] + weight_scratch,
        limit=57,
        micros=5,
        name="low_forward",
    )(pos, unshuffled, bottom_cond, cot, *weights)
    recv = to_all(send, ROWS)
    keys = row_devices * low_tokens
    (back,) = call(
        low_attend,
        [smem(), smem(), vmem()],
        [(exchange, bf16)],
        [
            pltpu.VMEM((keys, HEAD), bf16),
            pltpu.VMEM((2 * HEAD, keys), bf16),
            pltpu.VMEM((keys, 2 * HEAD), bf16),
            pltpu.VMEM((2 * HEAD, keys), bf16),
            pltpu.VMEM((keys, HEAD), f32),
            pltpu.VMEM((keys, 2 * HEAD), f32),
        ],
        micros=11,
        name="low_attend",
    )(pos, bottom_scale, recv)
    ret = to_all(back, ROWS)
    low_cols, merge_cols = 3 * width // images, width // images
    output, low_parts, grad_middle = call(
        low_backward,
        [smem()] + [vmem()] * 4 + [anywhere()] * len(weights),
        [
            ((low_tokens, width), bf16),
            ((images, low_tokens, low_cols + merge_cols), bf16),
            ((tokens, top), f32),
        ],
        [pltpu.VMEM((low_tokens, 3 * width), bf16), pltpu.VMEM((low_tokens, width), bf16)]
        + weight_scratch,
        limit=57,
        micros=6,
        name="low_backward",
    )(pos, ret, low, bottom_cond, cot, *weights)
    low_parts = to_all(low_parts, DP).reshape(images * low_tokens, low_cols + merge_cols)

    steps = images // 2
    part_rows = ext * 3 // 2
    top_pairs = top // (2 * HEAD)
    backward_scratch = [
        pltpu.VMEM((ext, tokens), f32),
        pltpu.VMEM((ext, 3 * top // 2), bf16),
        pltpu.VMEM((tokens, top // 2), f32),
        pltpu.VMEM((tokens, top // 2), f32),
        pltpu.SemaphoreType.DMA((5,)),
    ]
    (half_grad,) = call(
        functools.partial(top_backward, grid_rows, cols, 0),
        [smem(), smem(), vmem()] + [anywhere()] * 3,
        [((ext, 3 * top // 2), bf16)],
        backward_scratch,
        limit=56,
        micros=8,
        name="top_backward",
    )(pos, top_scale, grad_middle, proj, top_out, top_inv)

    top_all = lax.all_gather(top_ext, DP, axis=0, tiled=True)
    unsh_all = lax.all_gather(unshuffled, DP, axis=0, tiled=True)
    normed_all = lax.all_gather(low_normed, DP, axis=0, tiled=True)
    low_parts, half_grad = lax.optimization_barrier((low_parts, half_grad))
    (sums,) = call(
        product_low,
        [vmem()] + [anywhere()] * 2,
        [((row_devices, merge_rows + 3 * width // images * low_rows // 128, 128), bf16)],
        [
            pltpu.VMEM(unsh_all.shape, bf16),
            pltpu.VMEM(normed_all.shape, bf16),
            pltpu.SemaphoreType.DMA((8,)),
        ],
        limit=56,
        micros=4,
        name="product_low",
    )(low_parts, unsh_all, normed_all)
    sums, half_grad = lax.optimization_barrier((sums, half_grad))
    grad_ext_top, up, down, *mine, theirs = call(
        functools.partial(top_backward_rest, grid_rows, cols, top_pairs // 2),
        [smem(), smem(), vmem(), vmem()] + [anywhere()] * 3,
        [((ext, 3 * top), bf16)]
        + [((edge, 2 * top), bf16)] * 2
        + [((part_rows, 128), bf16)] * steps
        + [((steps, part_rows, 128), bf16)],
        [
            pltpu.VMEM((2, steps, part_rows, 128), bf16),
            pltpu.VMEM((ext, 3 * top // 2), bf16),
        ]
        + backward_scratch,
        limit=56,
        micros=8,
        name="top_backward_rest",
    )(pos, top_scale, grad_middle, half_grad, proj, top_out, top_inv)
    sums = to_all(sums, ROWS)

    def along_y(block, step):
        if step == 0:
            return block
        return lax.ppermute(block, "y", [(i, (i + step) % steps) for i in range(steps)])

    mine = [along_y(block, step) for step, block in enumerate(mine)]
    theirs = swap_cores(theirs)
    theirs = [along_y(theirs[step], step) for step in range(steps)]
    top_cols = 3 * top // images
    (part_top,) = call(
        product_top,
        [smem()] + [anywhere()] * (1 + images),
        [((row_devices, top // row_devices, top_cols), bf16)],
        [
            pltpu.VMEM((images * ext, 128), bf16),
            pltpu.VMEM((images * ext, 64), bf16),
            pltpu.VMEM(top_all.shape, bf16),
            pltpu.VMEM((images, part_rows, 128), bf16),
            pltpu.SemaphoreType.DMA((2 * images,)),
        ],
        limit=56,
        micros=3,
        name="product_top",
    )(pos, top_all, *[block for pair in zip(mine, theirs) for block in pair])
    from_next = lax.ppermute(up, ROWS, backward)
    from_prev = lax.ppermute(down, ROWS, forward)
    grad_ext_top, _ = lax.optimization_barrier((grad_ext_top, part_top))
    (grad_tokens,) = call(
        finish_tokens,
        [smem()] + [vmem()] * 8,
        [((tokens, top), bf16)],
        [pltpu.VMEM((tokens, 3 * top), bf16)],
        name="finish_tokens",
    )(pos, grad_ext_top, from_prev, from_next, tok, top_cond, grad_middle, top_own, top_other)
    part_top, sums = lax.optimization_barrier((part_top, sums))
    part_top = to_all(part_top, ROWS)
    sum_top = jnp.sum(part_top.astype(f32), axis=0)
    sums = jnp.sum(sums.astype(f32), axis=0)
    sum_merge = sums[:merge_rows]
    pieces = low_cols // 128
    sum_low = sums[merge_rows:].reshape(pieces, low_rows, 128).transpose(1, 0, 2)
    sum_low = sum_low.reshape(low_rows, pieces * 128)

    grad_tokens = grad_tokens.reshape(shard_rows, 2, cols // 2, top).transpose(0, 2, 1, 3)
    return (
        output.reshape(1, shard_rows // 2, cols // 2, width),
        grad_tokens.reshape(1, shard_rows, cols, top),
        sum_top,
        sum_merge,
        sum_low,
    )


def solution(mesh):
    images, row_devices = mesh.shape["dp"], mesh.shape["rows"]
    grid = mesh.devices.reshape(images // 2, 2, row_devices // 8, 8)
    split = Mesh(grid, ("y", "c", "x", "z"))
    placed = (
        P(DP, ROWS, None, None),
        P(DP, None),
        P(DP, None),
        P(ROWS, None),
        P(),
        P(ROWS, None),
        P(ROWS, None),
        P(),
        P(DP, ROWS, None, None),
    )
    return jax.shard_map(
        body,
        mesh=split,
        in_specs=placed,
        out_specs=(
            P(DP, ROWS, None, None),
            P(DP, ROWS, None, None),
            P(ROWS, DP),
            P(ROWS, DP),
            P(ROWS, DP),
        ),
        check_vma=False,
    )
```

```python
import functools
import jax
import jax.numpy as jnp
from jax import lax
from jax.experimental import pallas as pl
from jax.experimental.pallas import tpu as pltpu
from jax.sharding import Mesh, PartitionSpec as P

epsilon = 1e-06
log2e = 1.4426950408889634
f32 = jnp.float32
bf16 = jnp.bfloat16
ROWS = ("x", "z")
DP = ("y", "c")
HEAD = 64
MIB = 1 << 20
DP_STEPS = 4


def dot_nn(left, right):
    return jnp.dot(left, right, preferred_element_type=f32)


def dot_nt(left, right):
    return lax.dot_general(left, right, (((1,), (1,)), ((), ())), preferred_element_type=f32)


def dot_tn(left, right):
    return lax.dot_general(left, right, (((0,), (0,)), ((), ())), preferred_element_type=f32)


def unit_scale(x):
    return lax.rsqrt(jnp.mean(x * x, axis=-1, keepdims=True) + epsilon)


def unit_pull(x, scale, grad):
    inner = jnp.mean(x * grad, axis=-1, keepdims=True)
    return scale * grad - x * (scale * scale * scale * inner)


def grad_ext(grad, out):
    delta = jnp.sum(grad * out, axis=-1, keepdims=True)
    high = delta.astype(bf16).astype(f32)
    rest = delta - high
    lane = lax.broadcasted_iota(jnp.int32, grad.shape, 1)
    tail = jnp.where(lane == 0, -high, jnp.where(lane == 1, -rest, 0.0))
    return jnp.concatenate([grad, tail], axis=1).astype(bf16)


def vmem():
    return pl.BlockSpec(memory_space=pltpu.VMEM)


def smem():
    return pl.BlockSpec(memory_space=pltpu.SMEM)


def fetch(sources, targets, sems):
    copies = [
        pltpu.make_async_copy(source, target, sems.at[index])
        for index, (source, target) in enumerate(zip(sources, targets))
    ]
    for copy in copies:
        copy.start()
    return copies


def row_pieces(ref, count):
    rows = ref.shape[0] // count
    return [ref.at[i * rows : (i + 1) * rows] for i in range(count)]


def anywhere():
    return pl.BlockSpec(memory_space=pl.ANY)


def call(kernel, ins, outs, scratch=(), limit=40, micros=2, name=None):
    return pl.pallas_call(
        kernel,
        in_specs=ins,
        out_specs=[vmem() for _ in outs],
        out_shape=[jax.ShapeDtypeStruct(shape, kind) for shape, kind in outs],
        scratch_shapes=list(scratch),
        compiler_params=pltpu.CompilerParams(vmem_limit_bytes=limit * MIB),
        cost_estimate=pl.CostEstimate(
            flops=micros * 1000000000, bytes_accessed=micros * 3000000, transcendentals=0
        ),
        name=name,
    )


def neighbour_mask(first, grid_rows, cols, query_dim, shape):
    query = lax.broadcasted_iota(jnp.int32, shape, query_dim)
    key = lax.broadcasted_iota(jnp.int32, shape, 1 - query_dim)
    half = cols // 2

    def column(index):
        place = index % cols
        return 2 * (place % half) + place // half

    shift = key // cols - query // cols
    apart = column(key) - column(query)
    key_row = first - 3 + key // cols
    inside = (shift >= 0) & (shift <= 6) & (apart >= -3) & (apart <= 3)
    inside = inside & (key_row >= 0) & (key_row < grid_rows)
    return jnp.where(inside, 1.0, 0.0).astype(f32)


def head_parts(proj_ref, at, top, tokens):
    edge = (proj_ref.shape[0] - tokens) // 2
    query = proj_ref[edge : edge + tokens, at : at + HEAD].astype(f32)
    key = proj_ref[:, top + at : top + at + HEAD].astype(f32)
    value = proj_ref[:, 2 * top + at : 2 * top + at + HEAD]
    return query, key, value


def top_forward(
    grid_rows, cols, pos_ref, scale_ref, tok_ref, flat_ref, lo_ref, hi_ref, own_ref, other_ref,
    unsh_ref, out_ref, inv_ref, proj_ref, ext_ref, mask_ref,
):
    tokens, top = tok_ref.shape
    core = pos_ref[1]
    width = own_ref.shape[1]
    ext = jnp.concatenate([lo_ref[...], flat_ref[...], hi_ref[...]], axis=0)
    ext_ref[...] = ext
    here = pl.multiple_of(core * width, 128)
    there = pl.multiple_of((1 - core) * width, 128)
    proj_ref[:, pl.ds(here, width)] = dot_nn(ext, own_ref[...]).astype(bf16)
    proj_ref[:, pl.ds(there, width)] = dot_nn(ext, other_ref[...]).astype(bf16)
    mask_ref[...] = neighbour_mask(pos_ref[0], grid_rows, cols, 0, mask_ref.shape)
    for pair in range(top // (2 * HEAD)):
        heads = (2 * pair, 2 * pair + 1)
        parts = [head_parts(proj_ref, head * HEAD, top, tokens) for head in heads]
        queries = [
            (part[0] * (unit_scale(part[0]) * (scale_ref[head] * (log2e / HEAD)))).astype(bf16)
            for part, head in zip(parts, heads)
        ]
        keys = [(part[1] * unit_scale(part[1])).astype(bf16) for part in parts]
        scores = [dot_nt(query, key) for query, key in zip(queries, keys)]
        weights = [(jnp.exp2(score) * mask_ref[...]).astype(bf16) for score in scores]
        both = [
            dot_nn(weight, jnp.concatenate([part[2], jnp.ones_like(part[2])], axis=1))
            for weight, part in zip(weights, parts)
        ]
        invs = [1.0 / item[:, HEAD:] for item in both]
        outs = [item[:, :HEAD] * inverse for item, inverse in zip(both, invs)]
        at = pair * 2 * HEAD
        out_ref[:, at : at + 2 * HEAD] = jnp.concatenate(outs, axis=1)
        inv_ref[:, at : at + 2 * HEAD] = jnp.concatenate(invs, axis=1)
    half = cols // 2
    for row in range(tok_ref.shape[0] // cols):
        for odd in range(2):
            at = row * cols + odd * half
            part = tok_ref[at : at + half, :].astype(f32) + out_ref[at : at + half, :]
            low_at = (row // 2) * half
            place = (2 * (row % 2) + odd) * top
            unsh_ref[low_at : low_at + half, place : place + top] = part.astype(bf16)


def top_backward(
    grid_rows, cols, first_pair, pos_ref, scale_ref, grad_ref, proj_any, out_any, inv_any,
    whole_ref, mask_ref, proj_ref, out_ref, inv_ref, sems,
):
    tokens, width = out_ref.shape
    ext, top = whole_ref.shape[0], proj_any.shape[1] // 3
    start = first_pair * 2 * HEAD
    sources = [proj_any.at[:, i * top + start : i * top + start + width] for i in range(3)]
    sources += [ref.at[:, start : start + width] for ref in (out_any, inv_any)]
    targets = [proj_ref.at[:, i * width : (i + 1) * width] for i in range(3)]
    copies = fetch(sources, targets + [out_ref, inv_ref], sems)
    edge = (ext - tokens) // 2
    blank = jnp.zeros((edge, width), bf16)
    whole_ref[:edge, :width] = blank
    whole_ref[edge + tokens :, :width] = blank
    mask_ref[...] = neighbour_mask(pos_ref[0], grid_rows, cols, 1, mask_ref.shape)
    for copy in copies:
        copy.wait()
    for pair in range(width // (2 * HEAD)):
        heads = (2 * pair, 2 * pair + 1)
        parts = [head_parts(proj_ref, head * HEAD, width, tokens) for head in heads]
        gains = [scale_ref[2 * first_pair + head] * (1.0 / HEAD) for head in heads]
        query_scales = [unit_scale(query) for query, _, _ in parts]
        key_scales = [unit_scale(key) for _, key, _ in parts]
        query_units = [
            (part[0] * (scale * (gain * log2e))).astype(bf16)
            for part, scale, gain in zip(parts, query_scales, gains)
        ]
        keys = [part[1] * scale for part, scale in zip(parts, key_scales)]
        scores = [dot_nt(key.astype(bf16), query) for key, query in zip(keys, query_units)]
        grads = []
        for head in heads:
            at = head * HEAD
            grad = grad_ref[:, start + at : start + at + HEAD] * inv_ref[:, at : at + HEAD]
            grads.append(grad_ext(grad, out_ref[:, at : at + HEAD]))
        slopes = [
            dot_nt(jnp.concatenate([part[2], jnp.ones_like(part[2])], axis=1), grad)
            for part, grad in zip(parts, grads)
        ]
        weights = [jnp.exp2(score) * mask_ref[...] for score in scores]
        slopes = [(weight * slope).astype(bf16) for weight, slope in zip(weights, slopes)]
        key_ts = [
            jnp.concatenate([key, jnp.zeros_like(key)], axis=1).T.astype(bf16) for key in keys
        ]
        gvs = [
            dot_nn(weight.astype(bf16), grad)[:, :HEAD] for weight, grad in zip(weights, grads)
        ]
        gks = [dot_nn(slope, query) for slope, query in zip(slopes, query_units)]
        gqs = [dot_nn(key_t, slope) for key_t, slope in zip(key_ts, slopes)]
        gks = [
            unit_pull(part[1], scale, gk * (1.0 / log2e))
            for part, scale, gk in zip(parts, key_scales, gks)
        ]
        gqs = [
            unit_pull(part[0], scale, gq.T[:, :HEAD] * gain)
            for part, scale, gq, gain in zip(parts, query_scales, gqs, gains)
        ]
        at = pair * 2 * HEAD
        gq = jnp.concatenate(gqs, axis=1).astype(bf16)
        whole_ref[edge : edge + tokens, at : at + 2 * HEAD] = gq
        for base, grads in ((width + at, gks), (2 * width + at, gvs)):
            whole = jnp.concatenate(grads, axis=1).astype(bf16)
            whole_ref[:, base : base + 2 * HEAD] = whole


def top_backward_rest(
    grid_rows, cols, first_pair, pos_ref, scale_ref, grad_ref, prior_ref,
    proj_any, out_any, inv_any, whole_ref, up_ref, down_ref, *refs,
):
    mine, refs = refs[:DP_STEPS], refs[DP_STEPS:]
    theirs_ref, parts_s, here_s = refs[:3]
    top_backward(
        grid_rows, cols, first_pair, pos_ref, scale_ref, grad_ref, proj_any, out_any, inv_any,
        here_s, *refs[3:],
    )
    rows, width = here_s.shape[0], here_s.shape[1] // 3
    edge = up_ref.shape[0]
    top = 2 * width
    for block in range(3):
        for side, ref in enumerate((prior_ref, here_s)):
            at = (2 * block + side) * width
            whole_ref[:, at : at + width] = ref[:, block * width : (block + 1) * width]
    up_ref[...] = whole_ref[:edge, top:]
    down_ref[...] = whole_ref[rows - edge :, top:]
    part_cols = whole_ref.shape[1] // (2 * DP_STEPS)
    half = rows // 2
    for part in range(2 * DP_STEPS):
        step = lax.rem(part // 2 - pos_ref[4] + DP_STEPS, DP_STEPS)
        side = lax.rem(part + pos_ref[1], 2)
        at = part * part_cols
        parts_s[side, step, 0:rows, :] = whole_ref[:, at : at + 128]
        rest = whole_ref[:, at + 128 : at + part_cols]
        parts_s[side, step, rows:, :] = jnp.concatenate([rest[:half], rest[half:]], axis=1)
    for step in range(DP_STEPS):
        mine[step][...] = parts_s[0, step]
    theirs_ref[...] = parts_s[1]


def weight_copies(pos_ref, weights, merge_buf, low_buf, sems):
    steps_x, rows_low = low_buf.shape[1], low_buf.shape[3]
    steps_y = DP_STEPS
    rows = merge_buf.shape[3] // steps_y
    half_rows, cols = merge_buf.shape[3] // 2, merge_buf.shape[4] // 2
    merge, low = [[], []], [[], []]
    for side in range(2):
        for step in range(steps_y):
            place = lax.rem(pos_ref[4] + steps_y - step, steps_y) * rows
            merge[side].append(
                pltpu.make_async_copy(
                    weights[side * steps_y + step],
                    merge_buf.at[side, :, :, pl.ds(pl.multiple_of(place, rows), rows), 0:cols],
                    sems.at[side, step],
                )
            )
        rest = weights[2 * steps_y + side]
        for step in range(steps_x):
            place = lax.rem(pos_ref[3] + steps_x - step, steps_x)
            for part in range(2):
                merge[side].append(
                    pltpu.make_async_copy(
                        rest.at[:, step, rows_low:, part * cols : (part + 1) * cols],
                        merge_buf.at[
                            side, place, :, part * half_rows : (part + 1) * half_rows, cols:
                        ],
                        sems.at[side, steps_y + 3 * step + part],
                    )
                )
            low[side].append(
                pltpu.make_async_copy(
                    rest.at[:, step, 0:rows_low, :],
                    low_buf.at[side, place],
                    sems.at[side, steps_y + 3 * step + 2],
                )
            )
    return merge, low


def merge_block(merge_buf, side):
    part = merge_buf[side]
    return part.reshape(part.shape[0] * part.shape[1] * part.shape[2], part.shape[3])


def low_block(low_buf, side, block):
    rows = low_buf.shape[3] // 3
    part = low_buf[side, :, :, block * rows : (block + 1) * rows, :]
    return part.reshape(part.shape[0] * part.shape[1] * rows, part.shape[3])


def low_forward(pos_ref, unsh_ref, cond_ref, cot_ref, *refs):
    weights, (low_ref, normed_ref, send_ref, proj_s, merge_buf, low_buf, sems) = refs[:-7], refs[-7:]
    merge, lower = weight_copies(pos_ref, weights, merge_buf, low_buf, sems)
    for copy in merge[0] + merge[1] + lower[0] + lower[1]:
        copy.start()
    half = merge_buf.shape[4]
    width = 2 * half
    core = pos_ref[1]
    places = [core * half, (1 - core) * half]
    for side in range(2):
        for copy in merge[side]:
            copy.wait()
        place = pl.multiple_of(places[side], 128)
        low_ref[:, pl.ds(place, half)] = dot_nn(
            unsh_ref[...], merge_block(merge_buf, side)
        ).astype(bf16)
    low = low_ref[...].astype(f32)
    normed = (low * unit_scale(low) * cond_ref[...]).astype(bf16)
    normed_ref[...] = normed
    for side in range(2):
        for copy in lower[side]:
            copy.wait()
        for block in range(3):
            place = pl.multiple_of(block * width + places[side], 128)
            proj_s[:, pl.ds(place, half)] = dot_nn(
                normed, low_block(low_buf, side, block)
            ).astype(bf16)
    query, key, value = (proj_s[:, i * width : (i + 1) * width] for i in range(3))
    tokens = query.shape[0]
    share = tokens // 4
    for head in range(query.shape[1] // HEAD):
        at = head * HEAD
        key_value = jnp.concatenate([key[:, at : at + HEAD], value[:, at : at + HEAD]], axis=1)
        for part in range(2):
            send_ref[2 * head + part, 0:tokens, :] = key_value
            for index, rows in enumerate((query, cot_ref)):
                first = 2 * part * share
                send_ref[2 * head + part, tokens + index * share : tokens + (index + 1) * share] = (
                    jnp.concatenate(
                        [
                            rows[first : first + share, at : at + HEAD],
                            rows[first + share : first + 2 * share, at : at + HEAD],
                        ],
                        axis=1,
                    )
                )


def two_shares(ref_value):
    sources, share, lanes = ref_value.shape
    both = ref_value.reshape(sources * share, lanes).astype(f32)
    return jnp.concatenate([both[:, :HEAD], both[:, HEAD:]], axis=0)


def low_attend(
    pos_ref, scale_ref, recv_ref, back_ref, key_s, key_t_s, wide_s, wide_t_s, gk_s, gv_s,
):
    gain = scale_ref[pos_ref[2]] * (1.0 / HEAD)
    sources = recv_ref.shape[0]
    share = recv_ref.shape[1] // 6
    tokens = 4 * share
    keys = sources * tokens
    both = recv_ref[:, 0:tokens, :].reshape(keys, 2 * HEAD)
    key = both[:, :HEAD].astype(f32)
    key_scale = unit_scale(key)
    key_f = key * key_scale
    key_s[...] = key_f.astype(bf16)
    key_t_s[...] = jnp.concatenate([key_f, jnp.zeros_like(key_f)], axis=1).T.astype(bf16)
    wide = jnp.concatenate([both[:, HEAD:].astype(f32), jnp.ones_like(key_f)], axis=1)
    wide_s[...] = wide.astype(bf16)
    wide_t_s[...] = wide.T.astype(bf16)
    group = 8
    rows = group * share
    for block in range(sources // group):
        at = block * group
        query = two_shares(recv_ref[at : at + group, tokens : tokens + share, :])
        cot = two_shares(recv_ref[at : at + group, tokens + share :, :])
        query_scale = unit_scale(query)
        query_unit = (query * (query_scale * (gain * log2e))).astype(bf16)
        weight = jnp.exp2(dot_nt(key_s[...], query_unit)).astype(bf16)
        total = dot_nn(wide_t_s[...], weight).T
        inverse = 1.0 / total[:, HEAD:]
        out = total[:, :HEAD] * inverse
        grad = grad_ext(cot * inverse, out)
        slope = (weight.astype(f32) * dot_nt(wide_s[...], grad)).astype(bf16)
        gv = dot_nn(weight, grad)
        gk = dot_nn(slope, query_unit)
        if block == 0:
            gv_s[...] = gv
            gk_s[...] = gk
        else:
            gv_s[...] += gv
            gk_s[...] += gk
        gq = dot_nn(key_t_s[...], slope).T[:, :HEAD] * gain
        gq = unit_pull(query, query_scale, gq)
        result = jnp.concatenate([out, gq], axis=1).astype(bf16)
        for part in range(2):
            back_ref[at : at + group, tokens + part * share : tokens + (part + 1) * share, :] = (
                result[part * rows : (part + 1) * rows].reshape(group, share, 2 * HEAD)
            )
    gk = unit_pull(key, key_scale, gk_s[...] * (1.0 / log2e))
    result = jnp.concatenate([gk, gv_s[:, :HEAD]], axis=1).astype(bf16)
    back_ref[:, 0:tokens, :] = result.reshape(sources, tokens, 2 * HEAD)


def low_backward(pos_ref, ret_ref, low_ref, cond_ref, cot_ref, *refs):
    weights = refs[:-8]
    output_ref, parts_ref, gmid_ref, proj_s, grad_s, merge_buf, low_buf, sems = refs[-8:]
    merge, lower = weight_copies(pos_ref, weights, merge_buf, low_buf, sems)
    for copy in lower[0] + lower[1] + merge[0] + merge[1]:
        copy.start()
    half_width = merge_buf.shape[4]
    core = pos_ref[1]
    places = [core * half_width, (1 - core) * half_width]
    tokens, width = low_ref.shape
    share = tokens // 2
    low = low_ref[...].astype(f32)
    for pair in range(width // (2 * HEAD)):
        outs, gqs, gks, gvs = [], [], [], []
        for head in (2 * pair, 2 * pair + 1):
            first, second = ret_ref[2 * head], ret_ref[2 * head + 1]
            sums = first[:tokens].astype(f32) + second[:tokens].astype(f32)
            gks.append(sums[:, :HEAD])
            gvs.append(sums[:, HEAD:])
            query = jnp.concatenate([first[tokens:], second[tokens:]], axis=0)
            outs.append(query[:, :HEAD])
            gqs.append(query[:, HEAD:])
        at = pair * 2 * HEAD
        out = jnp.concatenate(outs, axis=1).astype(f32)
        output_ref[:, at : at + 2 * HEAD] = (low[:, at : at + 2 * HEAD] + out).astype(bf16)
        proj_s[:, at : at + 2 * HEAD] = jnp.concatenate(gqs, axis=1)
        proj_s[:, width + at : width + at + 2 * HEAD] = jnp.concatenate(gks, axis=1).astype(bf16)
        proj_s[:, 2 * width + at : 2 * width + at + 2 * HEAD] = jnp.concatenate(
            gvs, axis=1
        ).astype(bf16)
    groups = parts_ref.shape[0]
    low_cols = 3 * width // groups
    for part in range(groups):
        parts_ref[part, :, 0:low_cols] = proj_s[:, part * low_cols : (part + 1) * low_cols]
    back = jnp.zeros((tokens, width), f32)
    for side in range(2):
        for copy in lower[side]:
            copy.wait()
        for block in range(3):
            place = pl.multiple_of(block * width + places[side], 128)
            back = back + dot_nt(
                proj_s[:, pl.ds(place, half_width)], low_block(low_buf, side, block)
            )
    grad = unit_pull(low, unit_scale(low), back * cond_ref[...])
    grad_s[...] = (cot_ref[...].astype(f32) + grad).astype(bf16)
    merge_cols = width // groups
    for part in range(groups):
        parts_ref[part, :, low_cols:] = grad_s[:, part * merge_cols : (part + 1) * merge_cols]
    wide = jnp.zeros((tokens, 4 * gmid_ref.shape[1]), f32)
    for side in range(2):
        for copy in merge[side]:
            copy.wait()
        place = pl.multiple_of(places[side], 128)
        wide = wide + dot_nt(grad_s[:, pl.ds(place, half_width)], merge_block(merge_buf, side))
    top = gmid_ref.shape[1]
    half = 16
    for row in range(2 * tokens // half):
        for odd in range(2):
            at = (2 * row + odd) * half
            low_at = (row // 2) * half
            place = (2 * (row % 2) + odd) * top
            gmid_ref[at : at + half, :] = wide[low_at : low_at + half, place : place + top]


def product_low(parts_ref, unsh_ref, normed_ref, out_ref):
    devices = out_ref.shape[0]
    low_rows = normed_ref.shape[1] // devices
    merge_rows = unsh_ref.shape[1] // devices
    cols = parts_ref.shape[1] - 128
    part = dot_tn(unsh_ref[...], parts_ref[:, cols:]).astype(bf16)
    out_ref[:, 0:merge_rows, :] = part.reshape(devices, merge_rows, 128)
    part = dot_tn(normed_ref[...], parts_ref[:, :cols]).astype(bf16)
    for piece in range(cols // 128):
        at = merge_rows + piece * low_rows
        out_ref[:, at : at + low_rows, :] = part[:, piece * 128 : (piece + 1) * 128].reshape(
            devices, low_rows, 128
        )


def product_top(pos_ref, flat_any, *refs):
    blocks, out_ref, first_s, rest_s, flat_ref, blocks_s, sems = refs[:-6], *refs[-6:]
    steps = len(blocks) // 2
    count = len(blocks)
    copies = fetch(
        list(blocks) + row_pieces(flat_any, count),
        [blocks_s.at[index] for index in range(count)] + row_pieces(flat_ref, count),
        sems,
    )
    tokens = flat_ref.shape[0] // len(blocks)
    for step in range(steps):
        y = lax.rem(pos_ref[4] + steps - step, steps)
        for side in range(2):
            core = lax.rem(pos_ref[1] + side, 2)
            at = pl.multiple_of((2 * y + core) * tokens, 16)
            copies[2 * step + side].wait()
            block = blocks_s[2 * step + side]
            first_s[pl.ds(at, tokens), :] = block[0:tokens, :]
            rest = block[tokens:, :]
            rest_s[pl.ds(at, tokens), :] = jnp.concatenate([rest[:, :64], rest[:, 64:]], axis=0)
    devices = out_ref.shape[0]
    rows = flat_ref.shape[1] // devices
    both = jnp.concatenate([first_s[...], rest_s[...]], axis=1)
    for copy in copies[count:]:
        copy.wait()
    part = dot_tn(flat_ref[...], both).astype(bf16)
    out_ref[...] = part.reshape(devices, rows, part.shape[1])


def finish_tokens(
    pos_ref, whole_ref, prev_ref, next_ref, tok_ref, cond_ref, grad_ref, own_ref, other_ref,
    out_ref, sum_s,
):
    tokens, top = tok_ref.shape
    edge = prev_ref.shape[0]
    sum_s[...] = whole_ref[edge : edge + tokens, :]
    for at, ref in ((0, prev_ref), (tokens - edge, next_ref)):
        part = sum_s[at : at + edge, top:].astype(f32) + ref[...].astype(f32)
        sum_s[at : at + edge, top:] = part.astype(bf16)
    core = pos_ref[1]
    width = own_ref.shape[1]
    here = pl.multiple_of(core * width, 128)
    there = pl.multiple_of((1 - core) * width, 128)
    back = dot_nt(sum_s[:, pl.ds(here, width)], own_ref[...])
    back = back + dot_nt(sum_s[:, pl.ds(there, width)], other_ref[...])
    tok = tok_ref[...].astype(f32)
    out_ref[...] = (
        grad_ref[...] + unit_pull(tok, unit_scale(tok), back * cond_ref[...])
    ).astype(bf16)


def to_all(block, axis):
    return lax.all_to_all(block, axis, split_axis=0, concat_axis=0, tiled=True)


def spread(block, axis):
    count = lax.axis_size(axis)
    return lax.all_to_all(
        jnp.broadcast_to(block[None], (count,) + block.shape), axis, split_axis=0, concat_axis=0
    )


def around(block, axis):
    count = lax.axis_size(axis)
    return [block] + [
        lax.ppermute(block, axis, [(i, (i + step) % count) for i in range(count)])
        for step in range(1, count)
    ]


def swap_cores(block):
    return lax.ppermute(block, "c", [(0, 1), (1, 0)])


def body(
    image_tokens,
    top_cond,
    bottom_cond,
    top_qkv,
    top_scale,
    merge_weight,
    bottom_qkv,
    bottom_scale,
    out_cotangent,
):
    _, shard_rows, cols, top = image_tokens.shape
    width = bottom_cond.shape[1]
    row_devices = lax.axis_size(ROWS)
    images = lax.axis_size(DP)
    grid_rows = shard_rows * row_devices
    tokens = shard_rows * cols
    low_tokens = tokens // 4
    edge = 3 * cols
    row_at = lax.axis_index(ROWS)
    core = lax.axis_index("c")
    places = [row_at * shard_rows, core, row_at // 2, lax.axis_index("x"), lax.axis_index("y")]
    pos = jnp.stack(places).astype(jnp.int32)

    low_rows = bottom_qkv.shape[0]
    merge_rows = merge_weight.shape[0]
    half = width // 2
    merge_piece = lax.dynamic_slice_in_dim(merge_weight, core * half, half, 1)
    low_piece = jnp.concatenate(
        [bottom_qkv[:, i * width : (i + 1) * width] for i in range(3)], axis=0
    )
    low_piece = lax.dynamic_slice_in_dim(low_piece, core * half, half, 1)
    top_half = top_qkv.shape[1] // 2
    top_piece = lax.dynamic_slice_in_dim(top_qkv, core * top_half, top_half, 1)
    merge_side = merge_piece[:, half // 2 :]
    merge_side = jnp.concatenate(
        [merge_side[: merge_rows // 2], merge_side[merge_rows // 2 :]], axis=1
    )
    packed = jnp.stack(around(jnp.concatenate([low_piece, merge_side], axis=0), "x"))
    tok = image_tokens[0].reshape(shard_rows, cols // 2, 2, top).transpose(0, 2, 1, 3)
    tok = tok.reshape(tokens, top)
    tok_f = tok.astype(f32)
    top_flat = (tok_f * unit_scale(tok_f) * top_cond[0]).astype(bf16)
    forward = [(i, i + 1) for i in range(row_devices - 1)]
    backward = [(i + 1, i) for i in range(row_devices - 1)]
    lo = lax.ppermute(top_flat[tokens - edge :], ROWS, forward)
    hi = lax.ppermute(top_flat[:edge], ROWS, backward)
    packed = lax.optimization_barrier(packed)
    w_own = lax.all_gather(packed, "z", axis=0, tiled=False)
    steps = lax.axis_size("y")
    quarter = merge_rows // steps
    merge_piece = lax.dynamic_slice(
        merge_piece, (lax.axis_index("y") * quarter, 0), (quarter, half // 2)
    )
    first = jnp.concatenate([top_piece, merge_piece], axis=1)
    first, _ = lax.optimization_barrier((first, packed))
    first = spread(first, "z")
    first, lo, hi = lax.optimization_barrier((first, lo, hi))
    first = spread(first, "x")
    top_own = first[..., :top_half].reshape(top, top_half)
    top_other = swap_cores(top_own)
    merge_own = around(first[..., top_half:], "y")
    merge_other = [swap_cores(block) for block in merge_own]
    top_own, w_own, *merge_both = lax.optimization_barrier(
        (top_own, w_own, *merge_own, *merge_other)
    )

    ext = tokens + 2 * edge
    unshuffled, top_out, top_inv, proj, top_ext = call(
        functools.partial(top_forward, grid_rows, cols),
        [smem(), smem()] + [vmem()] * 6,
        [
            ((low_tokens, 4 * top), bf16),
            ((tokens, top), f32),
            ((tokens, top), f32),
            ((ext, 3 * top), bf16),
            ((ext, top), bf16),
        ],
        [pltpu.VMEM((tokens, ext), f32)],
        micros=6,
        name="top_forward",
    )(pos, top_scale, tok, top_flat, lo, hi, top_own, top_other)

    weights = (*merge_both, w_own, swap_cores(w_own))

    ring = (lax.axis_size("x"), lax.axis_size("z"))
    weight_scratch = [
        pltpu.VMEM((2,) + ring + (merge_rows, half), bf16),
        pltpu.VMEM((2,) + ring + (3 * low_rows, half), bf16),
        pltpu.SemaphoreType.DMA((2, steps + 3 * ring[0])),
    ]
    cot = out_cotangent[0].reshape(low_tokens, width)
    exchange = (row_devices, low_tokens * 3 // 2, 2 * HEAD)
    low, low_normed, send = call(
        low_forward,
        [smem()] + [vmem()] * 3 + [anywhere()] * len(weights),
        [((low_tokens, width), bf16), ((low_tokens, width), bf16), (exchange, bf16)],
        [pltpu.VMEM((low_tokens, 3 * width), bf16)] + weight_scratch,
        limit=57,
        micros=5,
        name="low_forward",
    )(pos, unshuffled, bottom_cond, cot, *weights)
    recv = to_all(send, ROWS)
    keys = row_devices * low_tokens
    (back,) = call(
        low_attend,
        [smem(), smem(), vmem()],
        [(exchange, bf16)],
        [
            pltpu.VMEM((keys, HEAD), bf16),
            pltpu.VMEM((2 * HEAD, keys), bf16),
            pltpu.VMEM((keys, 2 * HEAD), bf16),
            pltpu.VMEM((2 * HEAD, keys), bf16),
            pltpu.VMEM((keys, HEAD), f32),
            pltpu.VMEM((keys, 2 * HEAD), f32),
        ],
        micros=11,
        name="low_attend",
    )(pos, bottom_scale, recv)
    ret = to_all(back, ROWS)
    low_cols, merge_cols = 3 * width // images, width // images
    output, low_parts, grad_middle = call(
        low_backward,
        [smem()] + [vmem()] * 4 + [anywhere()] * len(weights),
        [
            ((low_tokens, width), bf16),
            ((images, low_tokens, low_cols + merge_cols), bf16),
            ((tokens, top), f32),
        ],
        [pltpu.VMEM((low_tokens, 3 * width), bf16), pltpu.VMEM((low_tokens, width), bf16)]
        + weight_scratch,
        limit=57,
        micros=6,
        name="low_backward",
    )(pos, ret, low, bottom_cond, cot, *weights)
    low_parts = to_all(low_parts, DP).reshape(images * low_tokens, low_cols + merge_cols)

    steps = images // 2
    part_rows = ext * 3 // 2
    top_pairs = top // (2 * HEAD)
    backward_scratch = [
        pltpu.VMEM((ext, tokens), f32),
        pltpu.VMEM((ext, 3 * top // 2), bf16),
        pltpu.VMEM((tokens, top // 2), f32),
        pltpu.VMEM((tokens, top // 2), f32),
        pltpu.SemaphoreType.DMA((5,)),
    ]
    (half_grad,) = call(
        functools.partial(top_backward, grid_rows, cols, 0),
        [smem(), smem(), vmem()] + [anywhere()] * 3,
        [((ext, 3 * top // 2), bf16)],
        backward_scratch,
        limit=56,
        micros=8,
        name="top_backward",
    )(pos, top_scale, grad_middle, proj, top_out, top_inv)

    top_all = lax.all_gather(top_ext, DP, axis=0, tiled=True)
    unsh_all = lax.all_gather(unshuffled, DP, axis=0, tiled=True)
    normed_all = lax.all_gather(low_normed, DP, axis=0, tiled=True)
    low_parts, half_grad = lax.optimization_barrier((low_parts, half_grad))
    (sums,) = call(
        product_low,
        [vmem()] * 3,
        [((row_devices, merge_rows + 3 * width // images * low_rows // 128, 128), bf16)],
        micros=3,
        name="product_low",
    )(low_parts, unsh_all, normed_all)
    sums, half_grad = lax.optimization_barrier((sums, half_grad))
    grad_ext_top, up, down, *mine, theirs = call(
        functools.partial(top_backward_rest, grid_rows, cols, top_pairs // 2),
        [smem(), smem(), vmem(), vmem()] + [anywhere()] * 3,
        [((ext, 3 * top), bf16)]
        + [((edge, 2 * top), bf16)] * 2
        + [((part_rows, 128), bf16)] * steps
        + [((steps, part_rows, 128), bf16)],
        [
            pltpu.VMEM((2, steps, part_rows, 128), bf16),
            pltpu.VMEM((ext, 3 * top // 2), bf16),
        ]
        + backward_scratch,
        limit=56,
        micros=8,
        name="top_backward_rest",
    )(pos, top_scale, grad_middle, half_grad, proj, top_out, top_inv)
    sums = to_all(sums, ROWS)

    def along_y(block, step):
        if step == 0:
            return block
        return lax.ppermute(block, "y", [(i, (i + step) % steps) for i in range(steps)])

    mine = [along_y(block, step) for step, block in enumerate(mine)]
    theirs = swap_cores(theirs)
    theirs = [along_y(theirs[step], step) for step in range(steps)]
    top_cols = 3 * top // images
    (part_top,) = call(
        product_top,
        [smem()] + [anywhere()] * (1 + images),
        [((row_devices, top // row_devices, top_cols), bf16)],
        [
            pltpu.VMEM((images * ext, 128), bf16),
            pltpu.VMEM((images * ext, 64), bf16),
            pltpu.VMEM(top_all.shape, bf16),
            pltpu.VMEM((images, part_rows, 128), bf16),
            pltpu.SemaphoreType.DMA((2 * images,)),
        ],
        limit=56,
        micros=3,
        name="product_top",
    )(pos, top_all, *[block for pair in zip(mine, theirs) for block in pair])
    from_next = lax.ppermute(up, ROWS, backward)
    from_prev = lax.ppermute(down, ROWS, forward)
    grad_ext_top, _ = lax.optimization_barrier((grad_ext_top, part_top))
    (grad_tokens,) = call(
        finish_tokens,
        [smem()] + [vmem()] * 8,
        [((tokens, top), bf16)],
        [pltpu.VMEM((tokens, 3 * top), bf16)],
        name="finish_tokens",
    )(pos, grad_ext_top, from_prev, from_next, tok, top_cond, grad_middle, top_own, top_other)
    part_top, sums = lax.optimization_barrier((part_top, sums))
    part_top = to_all(part_top, ROWS)
    sum_top = jnp.sum(part_top.astype(f32), axis=0)
    sums = jnp.sum(sums.astype(f32), axis=0)
    sum_merge = sums[:merge_rows]
    pieces = low_cols // 128
    sum_low = sums[merge_rows:].reshape(pieces, low_rows, 128).transpose(1, 0, 2)
    sum_low = sum_low.reshape(low_rows, pieces * 128)

    grad_tokens = grad_tokens.reshape(shard_rows, 2, cols // 2, top).transpose(0, 2, 1, 3)
    return (
        output.reshape(1, shard_rows // 2, cols // 2, width),
        grad_tokens.reshape(1, shard_rows, cols, top),
        sum_top,
        sum_merge,
        sum_low,
    )


def solution(mesh):
    images, row_devices = mesh.shape["dp"], mesh.shape["rows"]
    grid = mesh.devices.reshape(images // 2, 2, row_devices // 8, 8)
    split = Mesh(grid, ("y", "c", "x", "z"))
    placed = (
        P(DP, ROWS, None, None),
        P(DP, None),
        P(DP, None),
        P(ROWS, None),
        P(),
        P(ROWS, None),
        P(ROWS, None),
        P(),
        P(DP, ROWS, None, None),
    )
    return jax.shard_map(
        body,
        mesh=split,
        in_specs=placed,
        out_specs=(
            P(DP, ROWS, None, None),
            P(DP, ROWS, None, None),
            P(ROWS, DP),
            P(ROWS, DP),
            P(ROWS, DP),
        ),
        check_vma=False,
    )
```

```python
import functools
import jax
import jax.numpy as jnp
from jax import lax
from jax.experimental import pallas as pl
from jax.experimental.pallas import tpu as pltpu
from jax.sharding import Mesh, PartitionSpec as P

epsilon = 1e-06
log2e = 1.4426950408889634
f32 = jnp.float32
bf16 = jnp.bfloat16
ROWS = ("x", "z")
DP = ("y", "c")
HEAD = 64
MIB = 1 << 20
DP_STEPS = 4


def dot_nn(left, right):
    return jnp.dot(left, right, preferred_element_type=f32)


def dot_nt(left, right):
    return lax.dot_general(left, right, (((1,), (1,)), ((), ())), preferred_element_type=f32)


def dot_tn(left, right):
    return lax.dot_general(left, right, (((0,), (0,)), ((), ())), preferred_element_type=f32)


def unit_scale(x):
    return lax.rsqrt(jnp.mean(x * x, axis=-1, keepdims=True) + epsilon)


def unit_pull(x, scale, grad):
    inner = jnp.mean(x * grad, axis=-1, keepdims=True)
    return scale * grad - x * (scale * scale * scale * inner)


def grad_ext(grad, out):
    delta = jnp.sum(grad * out, axis=-1, keepdims=True)
    high = delta.astype(bf16).astype(f32)
    rest = delta - high
    lane = lax.broadcasted_iota(jnp.int32, grad.shape, 1)
    tail = jnp.where(lane == 0, -high, jnp.where(lane == 1, -rest, 0.0))
    return jnp.concatenate([grad, tail], axis=1).astype(bf16)


def vmem():
    return pl.BlockSpec(memory_space=pltpu.VMEM)


def smem():
    return pl.BlockSpec(memory_space=pltpu.SMEM)


def fetch(sources, targets, sems):
    copies = [
        pltpu.make_async_copy(source, target, sems.at[index])
        for index, (source, target) in enumerate(zip(sources, targets))
    ]
    for copy in copies:
        copy.start()
    return copies


def row_pieces(ref, count):
    rows = ref.shape[0] // count
    return [ref.at[i * rows : (i + 1) * rows] for i in range(count)]


def anywhere():
    return pl.BlockSpec(memory_space=pl.ANY)


def call(kernel, ins, outs, scratch=(), limit=40, micros=2, name=None):
    return pl.pallas_call(
        kernel,
        in_specs=ins,
        out_specs=[vmem() for _ in outs],
        out_shape=[jax.ShapeDtypeStruct(shape, kind) for shape, kind in outs],
        scratch_shapes=list(scratch),
        compiler_params=pltpu.CompilerParams(vmem_limit_bytes=limit * MIB),
        cost_estimate=pl.CostEstimate(
            flops=micros * 1000000000, bytes_accessed=micros * 3000000, transcendentals=0
        ),
        name=name,
    )


def neighbour_mask(first, grid_rows, cols, query_dim, shape):
    query = lax.broadcasted_iota(jnp.int32, shape, query_dim)
    key = lax.broadcasted_iota(jnp.int32, shape, 1 - query_dim)
    half = cols // 2

    def column(index):
        place = index % cols
        return 2 * (place % half) + place // half

    shift = key // cols - query // cols
    apart = column(key) - column(query)
    key_row = first - 3 + key // cols
    inside = (shift >= 0) & (shift <= 6) & (apart >= -3) & (apart <= 3)
    inside = inside & (key_row >= 0) & (key_row < grid_rows)
    return jnp.where(inside, 1.0, 0.0).astype(f32)


def head_parts(proj_ref, at, top, tokens):
    edge = (proj_ref.shape[0] - tokens) // 2
    query = proj_ref[edge : edge + tokens, at : at + HEAD].astype(f32)
    key = proj_ref[:, top + at : top + at + HEAD].astype(f32)
    value = proj_ref[:, 2 * top + at : 2 * top + at + HEAD]
    return query, key, value


def top_forward(
    grid_rows, cols, pos_ref, scale_ref, tok_ref, flat_ref, lo_ref, hi_ref, own_ref, other_ref,
    unsh_ref, out_ref, inv_ref, proj_ref, ext_ref, mask_ref,
):
    tokens, top = tok_ref.shape
    core = pos_ref[1]
    width = own_ref.shape[1]
    ext = jnp.concatenate([lo_ref[...], flat_ref[...], hi_ref[...]], axis=0)
    ext_ref[...] = ext
    here = pl.multiple_of(core * width, 128)
    there = pl.multiple_of((1 - core) * width, 128)
    proj_ref[:, pl.ds(here, width)] = dot_nn(ext, own_ref[...]).astype(bf16)
    proj_ref[:, pl.ds(there, width)] = dot_nn(ext, other_ref[...]).astype(bf16)
    mask_ref[...] = neighbour_mask(pos_ref[0], grid_rows, cols, 0, mask_ref.shape)
    for pair in range(top // (2 * HEAD)):
        heads = (2 * pair, 2 * pair + 1)
        parts = [head_parts(proj_ref, head * HEAD, top, tokens) for head in heads]
        queries = [
            (part[0] * (unit_scale(part[0]) * (scale_ref[head] * (log2e / HEAD)))).astype(bf16)
            for part, head in zip(parts, heads)
        ]
        keys = [(part[1] * unit_scale(part[1])).astype(bf16) for part in parts]
        scores = [dot_nt(query, key) for query, key in zip(queries, keys)]
        weights = [(jnp.exp2(score) * mask_ref[...]).astype(bf16) for score in scores]
        both = [
            dot_nn(weight, jnp.concatenate([part[2], jnp.ones_like(part[2])], axis=1))
            for weight, part in zip(weights, parts)
        ]
        invs = [1.0 / item[:, HEAD:] for item in both]
        outs = [item[:, :HEAD] * inverse for item, inverse in zip(both, invs)]
        at = pair * 2 * HEAD
        out_ref[:, at : at + 2 * HEAD] = jnp.concatenate(outs, axis=1)
        inv_ref[:, at : at + 2 * HEAD] = jnp.concatenate(invs, axis=1)
    half = cols // 2
    for row in range(tok_ref.shape[0] // cols):
        for odd in range(2):
            at = row * cols + odd * half
            part = tok_ref[at : at + half, :].astype(f32) + out_ref[at : at + half, :]
            low_at = (row // 2) * half
            place = (2 * (row % 2) + odd) * top
            unsh_ref[low_at : low_at + half, place : place + top] = part.astype(bf16)


def top_backward(
    grid_rows, cols, first_pair, pos_ref, scale_ref, grad_ref, proj_any, out_any, inv_any,
    whole_ref, mask_ref, proj_ref, out_ref, inv_ref, sems,
):
    tokens, width = out_ref.shape
    ext, top = whole_ref.shape[0], proj_any.shape[1] // 3
    start = first_pair * 2 * HEAD
    sources = [proj_any.at[:, i * top + start : i * top + start + width] for i in range(3)]
    sources += [ref.at[:, start : start + width] for ref in (out_any, inv_any)]
    targets = [proj_ref.at[:, i * width : (i + 1) * width] for i in range(3)]
    copies = fetch(sources, targets + [out_ref, inv_ref], sems)
    edge = (ext - tokens) // 2
    blank = jnp.zeros((edge, width), bf16)
    whole_ref[:edge, :width] = blank
    whole_ref[edge + tokens :, :width] = blank
    mask_ref[...] = neighbour_mask(pos_ref[0], grid_rows, cols, 1, mask_ref.shape)
    for copy in copies:
        copy.wait()
    for pair in range(width // (2 * HEAD)):
        heads = (2 * pair, 2 * pair + 1)
        parts = [head_parts(proj_ref, head * HEAD, width, tokens) for head in heads]
        gains = [scale_ref[2 * first_pair + head] * (1.0 / HEAD) for head in heads]
        query_scales = [unit_scale(query) for query, _, _ in parts]
        key_scales = [unit_scale(key) for _, key, _ in parts]
        query_units = [
            (part[0] * (scale * (gain * log2e))).astype(bf16)
            for part, scale, gain in zip(parts, query_scales, gains)
        ]
        keys = [part[1] * scale for part, scale in zip(parts, key_scales)]
        scores = [dot_nt(key.astype(bf16), query) for key, query in zip(keys, query_units)]
        grads = []
        for head in heads:
            at = head * HEAD
            grad = grad_ref[:, start + at : start + at + HEAD] * inv_ref[:, at : at + HEAD]
            grads.append(grad_ext(grad, out_ref[:, at : at + HEAD]))
        slopes = [
            dot_nt(jnp.concatenate([part[2], jnp.ones_like(part[2])], axis=1), grad)
            for part, grad in zip(parts, grads)
        ]
        weights = [jnp.exp2(score) * mask_ref[...] for score in scores]
        slopes = [(weight * slope).astype(bf16) for weight, slope in zip(weights, slopes)]
        key_ts = [
            jnp.concatenate([key, jnp.zeros_like(key)], axis=1).T.astype(bf16) for key in keys
        ]
        gvs = [
            dot_nn(weight.astype(bf16), grad)[:, :HEAD] for weight, grad in zip(weights, grads)
        ]
        gks = [dot_nn(slope, query) for slope, query in zip(slopes, query_units)]
        gqs = [dot_nn(key_t, slope) for key_t, slope in zip(key_ts, slopes)]
        gks = [
            unit_pull(part[1], scale, gk * (1.0 / log2e))
            for part, scale, gk in zip(parts, key_scales, gks)
        ]
        gqs = [
            unit_pull(part[0], scale, gq.T[:, :HEAD] * gain)
            for part, scale, gq, gain in zip(parts, query_scales, gqs, gains)
        ]
        at = pair * 2 * HEAD
        gq = jnp.concatenate(gqs, axis=1).astype(bf16)
        whole_ref[edge : edge + tokens, at : at + 2 * HEAD] = gq
        for base, grads in ((width + at, gks), (2 * width + at, gvs)):
            whole = jnp.concatenate(grads, axis=1).astype(bf16)
            whole_ref[:, base : base + 2 * HEAD] = whole


def top_backward_rest(
    grid_rows, cols, first_pair, pos_ref, scale_ref, grad_ref, prior_ref,
    proj_any, out_any, inv_any, whole_ref, up_ref, down_ref, *refs,
):
    mine, refs = refs[:DP_STEPS], refs[DP_STEPS:]
    theirs_ref, parts_s, here_s = refs[:3]
    top_backward(
        grid_rows, cols, first_pair, pos_ref, scale_ref, grad_ref, proj_any, out_any, inv_any,
        here_s, *refs[3:],
    )
    rows, width = here_s.shape[0], here_s.shape[1] // 3
    edge = up_ref.shape[0]
    top = 2 * width
    for block in range(3):
        for side, ref in enumerate((prior_ref, here_s)):
            at = (2 * block + side) * width
            whole_ref[:, at : at + width] = ref[:, block * width : (block + 1) * width]
    up_ref[...] = whole_ref[:edge, top:]
    down_ref[...] = whole_ref[rows - edge :, top:]
    part_cols = whole_ref.shape[1] // (2 * DP_STEPS)
    half = rows // 2
    for part in range(2 * DP_STEPS):
        step = lax.rem(part // 2 - pos_ref[4] + DP_STEPS, DP_STEPS)
        side = lax.rem(part + pos_ref[1], 2)
        at = part * part_cols
        parts_s[side, step, 0:rows, :] = whole_ref[:, at : at + 128]
        rest = whole_ref[:, at + 128 : at + part_cols]
        parts_s[side, step, rows:, :] = jnp.concatenate([rest[:half], rest[half:]], axis=1)
    for step in range(DP_STEPS):
        mine[step][...] = parts_s[0, step]
    theirs_ref[...] = parts_s[1]


def weight_copies(pos_ref, weights, merge_buf, low_buf, sems):
    steps_x, rows_low = low_buf.shape[1], low_buf.shape[3]
    steps_y = DP_STEPS
    rows = merge_buf.shape[3] // steps_y
    half_rows, cols = merge_buf.shape[3] // 2, merge_buf.shape[4] // 2
    merge, low = [[], []], [[], []]
    for side in range(2):
        for step in range(steps_y):
            place = lax.rem(pos_ref[4] + steps_y - step, steps_y) * rows
            merge[side].append(
                pltpu.make_async_copy(
                    weights[side * steps_y + step],
                    merge_buf.at[side, :, :, pl.ds(pl.multiple_of(place, rows), rows), 0:cols],
                    sems.at[side, step],
                )
            )
        rest = weights[2 * steps_y + side]
        for step in range(steps_x):
            place = lax.rem(pos_ref[3] + steps_x - step, steps_x)
            for part in range(2):
                merge[side].append(
                    pltpu.make_async_copy(
                        rest.at[:, step, rows_low:, part * cols : (part + 1) * cols],
                        merge_buf.at[
                            side, place, :, part * half_rows : (part + 1) * half_rows, cols:
                        ],
                        sems.at[side, steps_y + 3 * step + part],
                    )
                )
            low[side].append(
                pltpu.make_async_copy(
                    rest.at[:, step, 0:rows_low, :],
                    low_buf.at[side, place],
                    sems.at[side, steps_y + 3 * step + 2],
                )
            )
    return merge, low


def merge_block(merge_buf, side):
    part = merge_buf[side]
    return part.reshape(part.shape[0] * part.shape[1] * part.shape[2], part.shape[3])


def low_block(low_buf, side, block):
    rows = low_buf.shape[3] // 3
    part = low_buf[side, :, :, block * rows : (block + 1) * rows, :]
    return part.reshape(part.shape[0] * part.shape[1] * rows, part.shape[3])


def low_forward(pos_ref, unsh_ref, cond_ref, cot_ref, *refs):
    weights, (low_ref, normed_ref, send_ref, proj_s, merge_buf, low_buf, sems) = refs[:-7], refs[-7:]
    merge, lower = weight_copies(pos_ref, weights, merge_buf, low_buf, sems)
    for copy in merge[0] + merge[1] + lower[0] + lower[1]:
        copy.start()
    half = merge_buf.shape[4]
    width = 2 * half
    core = pos_ref[1]
    places = [core * half, (1 - core) * half]
    for side in range(2):
        for copy in merge[side]:
            copy.wait()
        place = pl.multiple_of(places[side], 128)
        low_ref[:, pl.ds(place, half)] = dot_nn(
            unsh_ref[...], merge_block(merge_buf, side)
        ).astype(bf16)
    low = low_ref[...].astype(f32)
    normed = (low * unit_scale(low) * cond_ref[...]).astype(bf16)
    normed_ref[...] = normed
    for side in range(2):
        for copy in lower[side]:
            copy.wait()
        for block in range(3):
            place = pl.multiple_of(block * width + places[side], 128)
            proj_s[:, pl.ds(place, half)] = dot_nn(
                normed, low_block(low_buf, side, block)
            ).astype(bf16)
    query, key, value = (proj_s[:, i * width : (i + 1) * width] for i in range(3))
    tokens = query.shape[0]
    share = tokens // 4
    for head in range(query.shape[1] // HEAD):
        at = head * HEAD
        key_value = jnp.concatenate([key[:, at : at + HEAD], value[:, at : at + HEAD]], axis=1)
        for part in range(2):
            send_ref[2 * head + part, 0:tokens, :] = key_value
            for index, rows in enumerate((query, cot_ref)):
                first = 2 * part * share
                send_ref[2 * head + part, tokens + index * share : tokens + (index + 1) * share] = (
                    jnp.concatenate(
                        [
                            rows[first : first + share, at : at + HEAD],
                            rows[first + share : first + 2 * share, at : at + HEAD],
                        ],
                        axis=1,
                    )
                )


def two_shares(ref_value):
    sources, share, lanes = ref_value.shape
    both = ref_value.reshape(sources * share, lanes).astype(f32)
    return jnp.concatenate([both[:, :HEAD], both[:, HEAD:]], axis=0)


def low_attend(
    pos_ref, scale_ref, recv_ref, back_ref, key_s, key_t_s, wide_s, wide_t_s, gk_s, gv_s,
):
    gain = scale_ref[pos_ref[2]] * (1.0 / HEAD)
    sources = recv_ref.shape[0]
    share = recv_ref.shape[1] // 6
    tokens = 4 * share
    keys = sources * tokens
    both = recv_ref[:, 0:tokens, :].reshape(keys, 2 * HEAD)
    key = both[:, :HEAD].astype(f32)
    key_scale = unit_scale(key)
    key_f = key * key_scale
    key_s[...] = key_f.astype(bf16)
    key_t_s[...] = jnp.concatenate([key_f, jnp.zeros_like(key_f)], axis=1).T.astype(bf16)
    wide = jnp.concatenate([both[:, HEAD:].astype(f32), jnp.ones_like(key_f)], axis=1)
    wide_s[...] = wide.astype(bf16)
    wide_t_s[...] = wide.T.astype(bf16)
    group = 8
    rows = group * share
    for block in range(sources // group):
        at = block * group
        query = two_shares(recv_ref[at : at + group, tokens : tokens + share, :])
        cot = two_shares(recv_ref[at : at + group, tokens + share :, :])
        query_scale = unit_scale(query)
        query_unit = (query * (query_scale * (gain * log2e))).astype(bf16)
        weight = jnp.exp2(dot_nt(key_s[...], query_unit)).astype(bf16)
        total = dot_nn(wide_t_s[...], weight).T
        inverse = 1.0 / total[:, HEAD:]
        out = total[:, :HEAD] * inverse
        grad = grad_ext(cot * inverse, out)
        slope = (weight.astype(f32) * dot_nt(wide_s[...], grad)).astype(bf16)
        gv = dot_nn(weight, grad)
        gk = dot_nn(slope, query_unit)
        if block == 0:
            gv_s[...] = gv
            gk_s[...] = gk
        else:
            gv_s[...] += gv
            gk_s[...] += gk
        gq = dot_nn(key_t_s[...], slope).T[:, :HEAD] * gain
        gq = unit_pull(query, query_scale, gq)
        result = jnp.concatenate([out, gq], axis=1).astype(bf16)
        for part in range(2):
            back_ref[at : at + group, tokens + part * share : tokens + (part + 1) * share, :] = (
                result[part * rows : (part + 1) * rows].reshape(group, share, 2 * HEAD)
            )
    gk = unit_pull(key, key_scale, gk_s[...] * (1.0 / log2e))
    result = jnp.concatenate([gk, gv_s[:, :HEAD]], axis=1).astype(bf16)
    back_ref[:, 0:tokens, :] = result.reshape(sources, tokens, 2 * HEAD)


def low_backward(pos_ref, ret_ref, low_ref, cond_ref, cot_ref, *refs):
    weights = refs[:-8]
    output_ref, parts_ref, gmid_ref, proj_s, grad_s, merge_buf, low_buf, sems = refs[-8:]
    merge, lower = weight_copies(pos_ref, weights, merge_buf, low_buf, sems)
    for copy in lower[0] + lower[1] + merge[0] + merge[1]:
        copy.start()
    half_width = merge_buf.shape[4]
    core = pos_ref[1]
    places = [core * half_width, (1 - core) * half_width]
    tokens, width = low_ref.shape
    share = tokens // 2
    low = low_ref[...].astype(f32)
    for pair in range(width // (2 * HEAD)):
        outs, gqs, gks, gvs = [], [], [], []
        for head in (2 * pair, 2 * pair + 1):
            first, second = ret_ref[2 * head], ret_ref[2 * head + 1]
            sums = first[:tokens].astype(f32) + second[:tokens].astype(f32)
            gks.append(sums[:, :HEAD])
            gvs.append(sums[:, HEAD:])
            query = jnp.concatenate([first[tokens:], second[tokens:]], axis=0)
            outs.append(query[:, :HEAD])
            gqs.append(query[:, HEAD:])
        at = pair * 2 * HEAD
        out = jnp.concatenate(outs, axis=1).astype(f32)
        output_ref[:, at : at + 2 * HEAD] = (low[:, at : at + 2 * HEAD] + out).astype(bf16)
        proj_s[:, at : at + 2 * HEAD] = jnp.concatenate(gqs, axis=1)
        proj_s[:, width + at : width + at + 2 * HEAD] = jnp.concatenate(gks, axis=1).astype(bf16)
        proj_s[:, 2 * width + at : 2 * width + at + 2 * HEAD] = jnp.concatenate(
            gvs, axis=1
        ).astype(bf16)
    groups = parts_ref.shape[0]
    low_cols = 3 * width // groups
    for part in range(groups):
        parts_ref[part, :, 0:low_cols] = proj_s[:, part * low_cols : (part + 1) * low_cols]
    back = jnp.zeros((tokens, width), f32)
    for side in range(2):
        for copy in lower[side]:
            copy.wait()
        for block in range(3):
            place = pl.multiple_of(block * width + places[side], 128)
            back = back + dot_nt(
                proj_s[:, pl.ds(place, half_width)], low_block(low_buf, side, block)
            )
    grad = unit_pull(low, unit_scale(low), back * cond_ref[...])
    grad_s[...] = (cot_ref[...].astype(f32) + grad).astype(bf16)
    merge_cols = width // groups
    for part in range(groups):
        parts_ref[part, :, low_cols:] = grad_s[:, part * merge_cols : (part + 1) * merge_cols]
    wide = jnp.zeros((tokens, 4 * gmid_ref.shape[1]), f32)
    for side in range(2):
        for copy in merge[side]:
            copy.wait()
        place = pl.multiple_of(places[side], 128)
        wide = wide + dot_nt(grad_s[:, pl.ds(place, half_width)], merge_block(merge_buf, side))
    top = gmid_ref.shape[1]
    half = 16
    for row in range(2 * tokens // half):
        for odd in range(2):
            at = (2 * row + odd) * half
            low_at = (row // 2) * half
            place = (2 * (row % 2) + odd) * top
            gmid_ref[at : at + half, :] = wide[low_at : low_at + half, place : place + top]


def product_low(parts_ref, unsh_ref, normed_ref, out_ref):
    devices = out_ref.shape[0]
    low_rows = normed_ref.shape[1] // devices
    merge_rows = unsh_ref.shape[1] // devices
    cols = parts_ref.shape[1] - 128
    part = dot_tn(unsh_ref[...], parts_ref[:, cols:]).astype(bf16)
    out_ref[:, 0:merge_rows, :] = part.reshape(devices, merge_rows, 128)
    part = dot_tn(normed_ref[...], parts_ref[:, :cols]).astype(bf16)
    for piece in range(cols // 128):
        at = merge_rows + piece * low_rows
        out_ref[:, at : at + low_rows, :] = part[:, piece * 128 : (piece + 1) * 128].reshape(
            devices, low_rows, 128
        )


def product_top(pos_ref, flat_any, *refs):
    blocks, out_ref, first_s, rest_s, flat_ref, blocks_s, sems = refs[:-6], *refs[-6:]
    steps = len(blocks) // 2
    count = len(blocks)
    copies = fetch(
        list(blocks) + row_pieces(flat_any, count),
        [blocks_s.at[index] for index in range(count)] + row_pieces(flat_ref, count),
        sems,
    )
    tokens = flat_ref.shape[0] // len(blocks)
    for step in range(steps):
        y = lax.rem(pos_ref[4] + steps - step, steps)
        for side in range(2):
            core = lax.rem(pos_ref[1] + side, 2)
            at = pl.multiple_of((2 * y + core) * tokens, 16)
            copies[2 * step + side].wait()
            block = blocks_s[2 * step + side]
            first_s[pl.ds(at, tokens), :] = block[0:tokens, :]
            rest = block[tokens:, :]
            rest_s[pl.ds(at, tokens), :] = jnp.concatenate([rest[:, :64], rest[:, 64:]], axis=0)
    devices = out_ref.shape[0]
    rows = flat_ref.shape[1] // devices
    both = jnp.concatenate([first_s[...], rest_s[...]], axis=1)
    for copy in copies[count:]:
        copy.wait()
    part = dot_tn(flat_ref[...], both).astype(bf16)
    out_ref[...] = part.reshape(devices, rows, part.shape[1])


def finish_tokens(
    pos_ref, whole_ref, prev_ref, next_ref, tok_ref, cond_ref, grad_ref, own_ref, other_ref,
    out_ref, sum_s,
):
    tokens, top = tok_ref.shape
    edge = prev_ref.shape[0]
    sum_s[...] = whole_ref[edge : edge + tokens, :]
    for at, ref in ((0, prev_ref), (tokens - edge, next_ref)):
        part = sum_s[at : at + edge, top:].astype(f32) + ref[...].astype(f32)
        sum_s[at : at + edge, top:] = part.astype(bf16)
    core = pos_ref[1]
    width = own_ref.shape[1]
    here = pl.multiple_of(core * width, 128)
    there = pl.multiple_of((1 - core) * width, 128)
    back = dot_nt(sum_s[:, pl.ds(here, width)], own_ref[...])
    back = back + dot_nt(sum_s[:, pl.ds(there, width)], other_ref[...])
    tok = tok_ref[...].astype(f32)
    out_ref[...] = (
        grad_ref[...] + unit_pull(tok, unit_scale(tok), back * cond_ref[...])
    ).astype(bf16)


def to_all(block, axis):
    return lax.all_to_all(block, axis, split_axis=0, concat_axis=0, tiled=True)


def spread(block, axis):
    count = lax.axis_size(axis)
    return lax.all_to_all(
        jnp.broadcast_to(block[None], (count,) + block.shape), axis, split_axis=0, concat_axis=0
    )


def around(block, axis):
    count = lax.axis_size(axis)
    return [block] + [
        lax.ppermute(block, axis, [(i, (i + step) % count) for i in range(count)])
        for step in range(1, count)
    ]


def swap_cores(block):
    return lax.ppermute(block, "c", [(0, 1), (1, 0)])


def body(
    image_tokens,
    top_cond,
    bottom_cond,
    top_qkv,
    top_scale,
    merge_weight,
    bottom_qkv,
    bottom_scale,
    out_cotangent,
):
    _, shard_rows, cols, top = image_tokens.shape
    width = bottom_cond.shape[1]
    row_devices = lax.axis_size(ROWS)
    images = lax.axis_size(DP)
    grid_rows = shard_rows * row_devices
    tokens = shard_rows * cols
    low_tokens = tokens // 4
    edge = 3 * cols
    row_at = lax.axis_index(ROWS)
    core = lax.axis_index("c")
    places = [row_at * shard_rows, core, row_at // 2, lax.axis_index("x"), lax.axis_index("y")]
    pos = jnp.stack(places).astype(jnp.int32)

    low_rows = bottom_qkv.shape[0]
    merge_rows = merge_weight.shape[0]
    half = width // 2
    merge_piece = lax.dynamic_slice_in_dim(merge_weight, core * half, half, 1)
    low_piece = jnp.concatenate(
        [bottom_qkv[:, i * width : (i + 1) * width] for i in range(3)], axis=0
    )
    low_piece = lax.dynamic_slice_in_dim(low_piece, core * half, half, 1)
    top_half = top_qkv.shape[1] // 2
    top_piece = lax.dynamic_slice_in_dim(top_qkv, core * top_half, top_half, 1)
    merge_side = merge_piece[:, half // 2 :]
    merge_side = jnp.concatenate(
        [merge_side[: merge_rows // 2], merge_side[merge_rows // 2 :]], axis=1
    )
    packed = jnp.stack(around(jnp.concatenate([low_piece, merge_side], axis=0), "x"))
    tok = image_tokens[0].reshape(shard_rows, cols // 2, 2, top).transpose(0, 2, 1, 3)
    tok = tok.reshape(tokens, top)
    tok_f = tok.astype(f32)
    top_flat = (tok_f * unit_scale(tok_f) * top_cond[0]).astype(bf16)
    forward = [(i, i + 1) for i in range(row_devices - 1)]
    backward = [(i + 1, i) for i in range(row_devices - 1)]
    lo = lax.ppermute(top_flat[tokens - edge :], ROWS, forward)
    hi = lax.ppermute(top_flat[:edge], ROWS, backward)
    packed = lax.optimization_barrier(packed)
    w_own = lax.all_gather(packed, "z", axis=0, tiled=False)
    steps = lax.axis_size("y")
    quarter = merge_rows // steps
    merge_piece = lax.dynamic_slice(
        merge_piece, (lax.axis_index("y") * quarter, 0), (quarter, half // 2)
    )
    first = jnp.concatenate([top_piece, merge_piece], axis=1)
    first = spread(first, "z")
    first, lo, hi = lax.optimization_barrier((first, lo, hi))
    first = spread(first, "x")
    top_own = first[..., :top_half].reshape(top, top_half)
    top_other = swap_cores(top_own)
    merge_own = around(first[..., top_half:], "y")
    merge_other = [swap_cores(block) for block in merge_own]
    top_own, w_own, *merge_both = lax.optimization_barrier(
        (top_own, w_own, *merge_own, *merge_other)
    )

    ext = tokens + 2 * edge
    unshuffled, top_out, top_inv, proj, top_ext = call(
        functools.partial(top_forward, grid_rows, cols),
        [smem(), smem()] + [vmem()] * 6,
        [
            ((low_tokens, 4 * top), bf16),
            ((tokens, top), f32),
            ((tokens, top), f32),
            ((ext, 3 * top), bf16),
            ((ext, top), bf16),
        ],
        [pltpu.VMEM((tokens, ext), f32)],
        micros=6,
        name="top_forward",
    )(pos, top_scale, tok, top_flat, lo, hi, top_own, top_other)

    weights = (*merge_both, w_own, swap_cores(w_own))

    ring = (lax.axis_size("x"), lax.axis_size("z"))
    weight_scratch = [
        pltpu.VMEM((2,) + ring + (merge_rows, half), bf16),
        pltpu.VMEM((2,) + ring + (3 * low_rows, half), bf16),
        pltpu.SemaphoreType.DMA((2, steps + 3 * ring[0])),
    ]
    cot = out_cotangent[0].reshape(low_tokens, width)
    exchange = (row_devices, low_tokens * 3 // 2, 2 * HEAD)
    low, low_normed, send = call(
        low_forward,
        [smem()] + [vmem()] * 3 + [anywhere()] * len(weights),
        [((low_tokens, width), bf16), ((low_tokens, width), bf16), (exchange, bf16)],
        [pltpu.VMEM((low_tokens, 3 * width), bf16)] + weight_scratch,
        limit=52,
        micros=5,
        name="low_forward",
    )(pos, unshuffled, bottom_cond, cot, *weights)
    recv = to_all(send, ROWS)
    keys = row_devices * low_tokens
    (back,) = call(
        low_attend,
        [smem(), smem(), vmem()],
        [(exchange, bf16)],
        [
            pltpu.VMEM((keys, HEAD), bf16),
            pltpu.VMEM((2 * HEAD, keys), bf16),
            pltpu.VMEM((keys, 2 * HEAD), bf16),
            pltpu.VMEM((2 * HEAD, keys), bf16),
            pltpu.VMEM((keys, HEAD), f32),
            pltpu.VMEM((keys, 2 * HEAD), f32),
        ],
        micros=11,
        name="low_attend",
    )(pos, bottom_scale, recv)
    ret = to_all(back, ROWS)
    low_cols, merge_cols = 3 * width // images, width // images
    output, low_parts, grad_middle = call(
        low_backward,
        [smem()] + [vmem()] * 4 + [anywhere()] * len(weights),
        [
            ((low_tokens, width), bf16),
            ((images, low_tokens, low_cols + merge_cols), bf16),
            ((tokens, top), f32),
        ],
        [pltpu.VMEM((low_tokens, 3 * width), bf16), pltpu.VMEM((low_tokens, width), bf16)]
        + weight_scratch,
        limit=57,
        micros=6,
        name="low_backward",
    )(pos, ret, low, bottom_cond, cot, *weights)
    low_parts = to_all(low_parts, DP).reshape(images * low_tokens, low_cols + merge_cols)

    steps = images // 2
    part_rows = ext * 3 // 2
    top_pairs = top // (2 * HEAD)
    backward_scratch = [
        pltpu.VMEM((ext, tokens), f32),
        pltpu.VMEM((ext, 3 * top // 2), bf16),
        pltpu.VMEM((tokens, top // 2), f32),
        pltpu.VMEM((tokens, top // 2), f32),
        pltpu.SemaphoreType.DMA((5,)),
    ]
    (half_grad,) = call(
        functools.partial(top_backward, grid_rows, cols, 0),
        [smem(), smem(), vmem()] + [anywhere()] * 3,
        [((ext, 3 * top // 2), bf16)],
        backward_scratch,
        limit=56,
        micros=8,
        name="top_backward",
    )(pos, top_scale, grad_middle, proj, top_out, top_inv)

    top_all = lax.all_gather(top_ext, DP, axis=0, tiled=True)
    unsh_all = lax.all_gather(unshuffled, DP, axis=0, tiled=True)
    normed_all = lax.all_gather(low_normed, DP, axis=0, tiled=True)
    low_parts, half_grad = lax.optimization_barrier((low_parts, half_grad))
    (sums,) = call(
        product_low,
        [vmem()] * 3,
        [((row_devices, merge_rows + 3 * width // images * low_rows // 128, 128), bf16)],
        micros=3,
        name="product_low",
    )(low_parts, unsh_all, normed_all)
    sums, half_grad = lax.optimization_barrier((sums, half_grad))
    grad_ext_top, up, down, *mine, theirs = call(
        functools.partial(top_backward_rest, grid_rows, cols, top_pairs // 2),
        [smem(), smem(), vmem(), vmem()] + [anywhere()] * 3,
        [((ext, 3 * top), bf16)]
        + [((edge, 2 * top), bf16)] * 2
        + [((part_rows, 128), bf16)] * steps
        + [((steps, part_rows, 128), bf16)],
        [
            pltpu.VMEM((2, steps, part_rows, 128), bf16),
            pltpu.VMEM((ext, 3 * top // 2), bf16),
        ]
        + backward_scratch,
        limit=56,
        micros=8,
        name="top_backward_rest",
    )(pos, top_scale, grad_middle, half_grad, proj, top_out, top_inv)
    sums = to_all(sums, ROWS)

    def along_y(block, step):
        if step == 0:
            return block
        return lax.ppermute(block, "y", [(i, (i + step) % steps) for i in range(steps)])

    mine = [along_y(block, step) for step, block in enumerate(mine)]
    theirs = swap_cores(theirs)
    theirs = [along_y(theirs[step], step) for step in range(steps)]
    top_cols = 3 * top // images
    (part_top,) = call(
        product_top,
        [smem()] + [anywhere()] * (1 + images),
        [((row_devices, top // row_devices, top_cols), bf16)],
        [
            pltpu.VMEM((images * ext, 128), bf16),
            pltpu.VMEM((images * ext, 64), bf16),
            pltpu.VMEM(top_all.shape, bf16),
            pltpu.VMEM((images, part_rows, 128), bf16),
            pltpu.SemaphoreType.DMA((2 * images,)),
        ],
        limit=56,
        micros=3,
        name="product_top",
    )(pos, top_all, *[block for pair in zip(mine, theirs) for block in pair])
    from_next = lax.ppermute(up, ROWS, backward)
    from_prev = lax.ppermute(down, ROWS, forward)
    grad_ext_top, _ = lax.optimization_barrier((grad_ext_top, part_top))
    (grad_tokens,) = call(
        finish_tokens,
        [smem()] + [vmem()] * 8,
        [((tokens, top), bf16)],
        [pltpu.VMEM((tokens, 3 * top), bf16)],
        name="finish_tokens",
    )(pos, grad_ext_top, from_prev, from_next, tok, top_cond, grad_middle, top_own, top_other)
    part_top, sums = lax.optimization_barrier((part_top, sums))
    part_top = to_all(part_top, ROWS)
    sum_top = jnp.sum(part_top.astype(f32), axis=0)
    sums = jnp.sum(sums.astype(f32), axis=0)
    sum_merge = sums[:merge_rows]
    pieces = low_cols // 128
    sum_low = sums[merge_rows:].reshape(pieces, low_rows, 128).transpose(1, 0, 2)
    sum_low = sum_low.reshape(low_rows, pieces * 128)

    grad_tokens = grad_tokens.reshape(shard_rows, 2, cols // 2, top).transpose(0, 2, 1, 3)
    return (
        output.reshape(1, shard_rows // 2, cols // 2, width),
        grad_tokens.reshape(1, shard_rows, cols, top),
        sum_top,
        sum_merge,
        sum_low,
    )


def solution(mesh):
    images, row_devices = mesh.shape["dp"], mesh.shape["rows"]
    grid = mesh.devices.reshape(images // 2, 2, row_devices // 8, 8)
    split = Mesh(grid, ("y", "c", "x", "z"))
    placed = (
        P(DP, ROWS, None, None),
        P(DP, None),
        P(DP, None),
        P(ROWS, None),
        P(),
        P(ROWS, None),
        P(ROWS, None),
        P(),
        P(DP, ROWS, None, None),
    )
    return jax.shard_map(
        body,
        mesh=split,
        in_specs=placed,
        out_specs=(
            P(DP, ROWS, None, None),
            P(DP, ROWS, None, None),
            P(ROWS, DP),
            P(ROWS, DP),
            P(ROWS, DP),
        ),
        check_vma=False,
    )
```
